256 devices in a mesh: seq: 8 (over y_hi, x), mp: 32 (over y_lo, z, core).
Axes of the slice: x: 4, y: 4 (y_hi: 2, y_lo: 2; y = y_hi * 2 + y_lo), z: 8, core: 2. Of those that a mesh axis runs over, the one named last changes fastest.
Arguments:
- tokens: bfloat16 [768, 8192], P('mp', 'seq'), may hold values from -6 to 6
- gate_weight: bfloat16 [8192, 28672], P('seq', 'mp'), may hold values from -0.09375 to 0.09375
- up_weight: bfloat16 [8192, 28672], P('seq', 'mp'), may hold values from -0.09375 to 0.09375
- down_weight: bfloat16 [28672, 8192], P('mp', 'seq'), may hold values from -0.046875 to 0.046875
- gate_mask: int32 [64, 224], P('seq', 'mp'), may hold values 0 or 1
- up_mask: int32 [64, 224], P('seq', 'mp'), may hold values 0 or 1
- down_mask: int32 [224, 64], P('mp', 'seq'), may hold values 0 or 1
- grad_out: bfloat16 [768, 8192], P('mp', 'seq'), may hold values from -6 to 6
Outputs:
- mixed: bfloat16 [768, 8192], P('mp', 'seq')
- grad_tokens: bfloat16 [768, 8192], P('mp', 'seq')
- grad_gate: bfloat16 [8192, 28672], P('seq', 'mp')
- grad_up: bfloat16 [8192, 28672], P('seq', 'mp')
- grad_down: bfloat16 [28672, 8192], P('mp', 'seq')
The draws below stay inside these ranges and needn't reach their ends.
All inputs are finite; a program needn't handle non-finite values. No bound on the sum of `gate_mask` or of `up_mask` or of `down_mask` on one device may be relied on, other than what follows from the above.
Results may differ from the reference program's by a relative error of at most 0.027.
Values may be sent and summed in bfloat16 or wider, within the bound.
A program may use at most 128 MiB of HBM per device.

```python
import math
import jax
import jax.numpy as jnp
from jax import lax

D = 8192
FF = 28672
BLK = 128
TOKENS = 768
N_SEQ = 8


def touch_ends(values, stream_key, low, high):
    index_at = [jax.random.randint(jax.random.fold_in(stream_key, axis), (), 0, length) for axis, length in enumerate(values.shape)]
    main_axis = values.shape.index(max(values.shape))
    next_to = index_at[:main_axis] + [(index_at[main_axis] + 1) % values.shape[main_axis]] + index_at[main_axis + 1:]
    return values.at[tuple(index_at)].set(low).at[tuple(next_to)].set(high)


def block_scale(rng, extent, split, least, top_value):
    gain = 1.0
    for axis_at, parts in split:
        draws = jax.random.uniform(jax.random.fold_in(jax.random.fold_in(rng, 6), axis_at), (parts,), jnp.float32, least / len(split), top_value / len(split))
        gain = gain * jnp.repeat(jnp.exp(draws), extent[axis_at] // parts).reshape((-1,) + (1,) * (len(extent) - 1 - axis_at))
    return gain


def centred(key, extent, deviation, reach, pieces=(), kind=jnp.bfloat16):
    loudness = block_scale(key, extent, pieces, -0.22, 0.18) if pieces else 1.0
    result = jax.random.normal(key, extent, jnp.float32) * deviation * loudness
    return jnp.minimum(jnp.maximum(result, -reach), reach).astype(kind)


def setup_inputs(seed: int = 0) -> dict:
    keys = jax.random.split(jax.random.key(seed), 9)
    tokens = centred(keys[0], (TOKENS, D), 1.0, 6.0, ((0, 32), (1, 8)))
    gate_weight = centred(keys[1], (D, FF), (D // 2) ** -0.5, 0.09375, ((0, 8), (1, 32)))
    up_weight = centred(keys[2], (D, FF), (D // 2) ** -0.5, 0.09375, ((0, 8), (1, 32)))
    down_weight = centred(keys[3], (FF, D), (FF // 2) ** -0.5, 0.046875, ((0, 32), (1, 8)))
    gate_mask = touch_ends((jax.random.randint(keys[4], (D // BLK, FF // BLK), 0, 2) < 1).astype(jnp.int32), jax.random.fold_in(keys[4], 1), 0, 1)
    up_mask = touch_ends((jax.random.randint(keys[5], (D // BLK, FF // BLK), 0, 2) < 1).astype(jnp.int32), jax.random.fold_in(keys[5], 1), 0, 1)
    down_mask = touch_ends((jax.random.randint(keys[6], (FF // BLK, D // BLK), 0, 2) < 1).astype(jnp.int32), jax.random.fold_in(keys[6], 1), 0, 1)
    grad_out = centred(keys[7], (TOKENS, D), 1.0, 6.0, ((0, 32), (1, 8)))
    return {"tokens": tokens, "gate_weight": gate_weight, "up_weight": up_weight, "down_weight": down_weight, "gate_mask": gate_mask, "up_mask": up_mask, "down_mask": down_mask, "grad_out": grad_out}


def apply_mask(weight, mask):
    block_rows, block_cols = mask.shape
    shaped = weight.reshape(block_rows, weight.shape[0] // block_rows, block_cols, weight.shape[1] // block_cols)
    return (shaped * mask.astype(weight.dtype)[:, None, :, None]).reshape(weight.shape)

def inner_left(left, right):
    return lax.dot_general(left, right, (((0,), (0,)), ((), ())), preferred_element_type=jnp.float32)

def inner_right(left, right):
    return lax.dot_general(left, right, (((1,), (1,)), ((), ())), preferred_element_type=jnp.float32)

def sliced_sum(left, right, transposed):
    width = left.shape[1] // N_SEQ
    total = None
    for index in range(N_SEQ):
        left_slice = left[:, index * width:(index + 1) * width]
        if transposed:
            term = inner_right(left_slice, right[:, index * width:(index + 1) * width])
        else:
            term = jnp.dot(left_slice, right[index * width:(index + 1) * width, :], preferred_element_type=jnp.float32)
        term = lax.optimization_barrier(term.astype(jnp.bfloat16)).astype(jnp.float32)
        total = term if total is None else total + term
    return total

def reference(tokens, gate_weight, up_weight, down_weight, gate_mask, up_mask, down_mask, grad_out):
    w_gate = apply_mask(gate_weight, gate_mask)
    w_up = apply_mask(up_weight, up_mask)
    w_down = apply_mask(down_weight, down_mask)
    grad_scale = 1.0 / math.sqrt(TOKENS)
    pre_gate = sliced_sum(tokens, w_gate, False)
    pre_up = sliced_sum(tokens, w_up, False)
    sig_gate = jax.nn.sigmoid(pre_gate)
    silu_gate = pre_gate * sig_gate
    hidden = (silu_gate * pre_up).astype(jnp.bfloat16)
    mixed = jnp.dot(hidden, w_down, preferred_element_type=jnp.float32).astype(jnp.bfloat16)
    grad_hidden = sliced_sum(grad_out, w_down, True)
    grad_pre_gate = (grad_hidden * pre_up * sig_gate * (1.0 + pre_gate * (1.0 - sig_gate))).astype(jnp.bfloat16)
    grad_pre_up = (grad_hidden * silu_gate).astype(jnp.bfloat16)
    grad_down = apply_mask(inner_left(hidden, grad_out) * grad_scale, down_mask).astype(jnp.bfloat16)
    grad_gate = apply_mask(inner_left(tokens, grad_pre_gate) * grad_scale, gate_mask).astype(jnp.bfloat16)
    grad_up = apply_mask(inner_left(tokens, grad_pre_up) * grad_scale, up_mask).astype(jnp.bfloat16)
    grad_tokens = (inner_right(grad_pre_gate, w_gate) + inner_right(grad_pre_up, w_up)).astype(jnp.bfloat16)
    return (mixed, grad_tokens, grad_gate, grad_up, grad_down)
```

```python
import functools
import math

import jax
import jax.numpy as jnp
from jax import lax
from jax.experimental import pallas as pl
from jax.experimental.pallas import tpu as pltpu
from jax.sharding import PartitionSpec as P

MESH = pl.DeviceIdType.MESH
BF = jnp.bfloat16
F32 = jnp.float32

TOK = 768
W = 1024
FH = 896
OWN = 24
CH = 48
R = 256
NCH = TOK // R
PR = R // 8
XR = R // 4
CA = 512
DZ = (1, 7, 2, 4, 3, 5, 6, 0)
NEG = tuple(DZ.index((8 - d) % 8) for d in DZ)
SELF = DZ.index(0)
NEED = [-(-(j + 1) * R // 96) for j in range(NCH)]
DONE = [0] + [((j + 1) * R) // 96 for j in range(NCH)]


def dot_nn(a, b):
    return jnp.dot(a, b, preferred_element_type=F32)


def dot_nt(a, b):
    return lax.dot_general(a, b, (((1,), (1,)), ((), ())), preferred_element_type=F32)


def dot_tn(a, b):
    return lax.dot_general(a, b, (((0,), (0,)), ((), ())), preferred_element_type=F32)


def loop(n, body):
    lax.fori_loop(0, n, lambda i, c: (body(i), c)[1], 0)


def kernel(
    tok_in, gw_in, uw_in, dw_in, gm, um, dm, cot_in,
    mix_out, gt_out, gg_out, gu_out, gd_out,
    wcat, wd, io_buf, slot_o, slot_s, tok, cot,
    p_gu, p_h, f1g, f1u, f2g, f2u, own_gu, sy_gu, fy_gu, fy_h, f1a, f1b, f2h,
    hid, gp, e_own, e_sib, e_sb, e_sr, ey_s, ey_r, ez_s, ez_r,
    lsem, ssem, rsem,
):
    s = lax.axis_index("seq")
    m = lax.axis_index("mp")
    h, x = s // 4, s % 4
    l, z, c = m // 16, (m // 2) % 8, m % 2
    xr, xl, xf = (x + 1) % 4, (x + 3) % 4, (x + 2) % 4
    oh = 1 - h

    def mp_of(dz, dl, dc=0):
        return ((l + dl) % 2) * 16 + ((z + dz) % 8) * 2 + (c + dc) % 2

    RIGHT, LEFT, YH = (h * 4 + xr, m), (h * 4 + xl, m), (oh * 4 + x, m)
    SIB, YL = (s, mp_of(0, 0, 1)), (s, mp_of(0, 1))

    def ZL(dz, dl):
        return (s, mp_of(dz, dl))

    ids, sent = {}, {}

    def send(key, src, dst, to):
        k = ids.setdefault(key, len(ids))
        d = pltpu.make_async_remote_copy(
            src_ref=src, dst_ref=dst, send_sem=ssem.at[k], recv_sem=rsem.at[k],
            device_id=to, device_id_type=MESH,
        )
        d.start()
        sent[key] = d

    def got(*keys):
        for key in keys:
            sent[key].wait_recv()

    loads = [
        pltpu.make_async_copy(tok_in, io_buf.at[0], lsem.at[0]),
        pltpu.make_async_copy(cot_in, io_buf.at[1], lsem.at[1]),
        pltpu.make_async_copy(gw_in, wcat.at[:, pl.ds(0, FH)], lsem.at[2]),
        pltpu.make_async_copy(uw_in, wcat.at[:, pl.ds(FH, FH)], lsem.at[3]),
        pltpu.make_async_copy(dw_in, wd, lsem.at[4]),
    ]
    for d in loads:
        d.start()

    barrier = pltpu.get_barrier_semaphore()
    peers = [RIGHT, LEFT, YH, SIB] + [
        ZL(dz, dl) for dz in range(8) for dl in range(2) if (dz, dl) != (0, 0)
    ]
    for to in peers:
        pl.semaphore_signal(barrier, inc=1, device_id=to, device_id_type=MESH)

    def pack(v):
        v = v.astype(F32)
        return jnp.concatenate([v[:, :512], v[:, 512:]], axis=0).astype(BF)

    def unpack(v):
        v = v.astype(F32)
        return jnp.concatenate([v[:OWN], v[OWN:]], axis=1)

    for a in range(2):
        loads[a].wait()
        slot_o[SELF, 0, a] = pack(io_buf[a])
    pl.semaphore_wait(barrier, len(peers))

    for q in range(8):
        p = NEG[q]
        for dl in range(2):
            if (DZ[p], dl) != (0, 0):
                send(("ag", q, dl), slot_o.at[SELF, 0], slot_o.at[q, dl], ZL(DZ[p], dl))

    def masked(w, ref, mask, rows, cols, col0):
        def body(i):
            r = pl.ds(pl.multiple_of(i * 128, 128), 128)
            for k in range(cols):
                cs = pl.ds(col0 + k * 128, 128)
                ref[r, cs] = (ref[r, cs].astype(F32) * mask[i, k].astype(F32)).astype(BF)
        loop(rows, body)

    loads[2].wait()
    masked(None, wcat, gm, 8, 7, 0)
    loads[3].wait()
    masked(None, wcat, um, 8, 7, FH)
    loads[4].wait()
    masked(None, wd, dm, 7, 8, 0)

    def share(q):
        for dl in range(2):
            if (DZ[q], dl) != (0, 0):
                got(("ag", q, dl))
        send(("sh", q), slot_o.at[q], slot_s.at[q], SIB)

    def assemble(q):
        got(("sh", q))
        for a, ref in ((0, tok), (1, cot)):
            for dl in range(2):
                v = jnp.concatenate([unpack(slot_o[q, dl, a]), unpack(slot_s[q, dl, a])], axis=0)
                ref[pl.ds(q * 96 + dl * CH, CH), :] = v.astype(BF)

    def rows_x(j, xi):
        return pl.ds(pl.multiple_of(j * R + xi * XR, XR), XR)

    def rows_p(j, xi, hi):
        return pl.ds(pl.multiple_of(j * R + xi * XR + hi * PR, PR), PR)

    G, U = pl.ds(0, FH), pl.ds(FH, FH)
    A, B = pl.ds(0, CA), pl.ds(CA, FH - CA)

    def part(j):
        rows = pl.ds(j * R, R)

        def body(n):
            cs = pl.ds(pl.multiple_of(n * 256, 256), 256)
            p_gu[rows, cs] = dot_nn(tok[rows, :], wcat[:, cs]).astype(BF)
        loop(7, body)
        send(("g1", j), p_gu.at[rows_x(j, xf), G], f1g.at[j], RIGHT)
        send(("u1", j), p_gu.at[rows_x(j, xf), U], f1u.at[j], LEFT)
        send(("g2l", j), p_gu.at[rows_x(j, xl), G], f2g.at[j, 1], LEFT)
        send(("u2r", j), p_gu.at[rows_x(j, xr), U], f2u.at[j, 0], RIGHT)

        def hbody(n):
            cs = pl.ds(pl.multiple_of(n * 256, 256), 256)
            v = dot_nt(cot[rows, :], wd[cs, :]).astype(BF)
            p_h[j, :, :, :, cs] = v.reshape(4, 2, PR, 256)
        loop(3, hbody)
        cs = pl.ds(768, 128)
        p_h[j, :, :, :, cs] = dot_nt(cot[rows, :], wd[cs, :]).astype(BF).reshape(4, 2, PR, 128)
        send(("hy", j), p_h.at[j, :, oh], fy_h.at[j], YH)

    def r1(j):
        got(("g1", j))
        rows = rows_x(j, xr)
        p_gu[rows, G] = (p_gu[rows, G].astype(F32) + f1g[j].astype(F32)).astype(BF)
        send(("g2r", j), p_gu.at[rows, G], f2g.at[j, 0], RIGHT)
        got(("u1", j))
        rows = rows_x(j, xl)
        p_gu[rows, U] = (p_gu[rows, U].astype(F32) + f1u[j].astype(F32)).astype(BF)
        send(("u2l", j), p_gu.at[rows, U], f2u.at[j, 1], LEFT)
        got(("hy", j))
        for xi in range(4):
            p_h[j, xi, h] = (p_h[j, xi, h].astype(F32) + fy_h[j, xi].astype(F32)).astype(BF)
        send(("h1a", j), p_h.at[j, xf, h, :, A], f1a.at[j], RIGHT)
        send(("h1b", j), p_h.at[j, xf, h, :, B], f1b.at[j], LEFT)
        send(("h2rb", j), p_h.at[j, xr, h, :, B], f2h.at[j, 0, :, B], RIGHT)
        send(("h2la", j), p_h.at[j, xl, h, :, A], f2h.at[j, 1, :, A], LEFT)

    def r2(j):
        got(("h1a", j))
        p_h[j, xr, h, :, A] = (p_h[j, xr, h, :, A].astype(F32) + f1a[j].astype(F32)).astype(BF)
        send(("h2ra", j), p_h.at[j, xr, h, :, A], f2h.at[j, 0, :, A], RIGHT)
        got(("h1b", j))
        p_h[j, xl, h, :, B] = (p_h[j, xl, h, :, B].astype(F32) + f1b[j].astype(F32)).astype(BF)
        send(("h2lb", j), p_h.at[j, xl, h, :, B], f2h.at[j, 1, :, B], LEFT)
        got(("g2l", j), ("u2r", j), ("g2r", j), ("u2l", j))
        for f2, cs in ((f2g, G), (f2u, U)):
            def total(hi):
                r = pl.ds(pl.multiple_of(hi * PR, PR), PR)
                return (
                    p_gu[rows_p(j, x, hi), cs].astype(F32)
                    + f2[j, 0, r, :].astype(F32)
                    + f2[j, 1, r, :].astype(F32)
                )
            sy_gu[j, :, cs] = total(oh).astype(BF)
            own_gu[j, :, cs] = total(h)
        send(("guy", j), sy_gu.at[j], fy_gu.at[j], YH)

    def r3(j):
        got(("guy", j), ("h2rb", j), ("h2la", j), ("h2ra", j), ("h2lb", j))
        mine = rows_p(j, x, h)
        step = 16

        def body(i):
            r = pl.ds(pl.multiple_of(i * step, step), step)
            pre_gate = own_gu[j, r, G] + fy_gu[j, r, G].astype(F32)
            pre_up = own_gu[j, r, U] + fy_gu[j, r, U].astype(F32)
            grad_hidden = (
                p_h[j, x, h, r, :].astype(F32) + f2h[j, 0, r, :].astype(F32) + f2h[j, 1, r, :].astype(F32)
            )
            sig = jax.nn.sigmoid(pre_gate)
            silu = pre_gate * sig
            rr = pl.ds(pl.multiple_of(j * R + x * XR + h * PR + i * step, step), step)
            hid[rr, :] = (silu * pre_up).astype(BF)
            gp[rr, G] = (grad_hidden * pre_up * sig * (1.0 + pre_gate * (1.0 - sig))).astype(BF)
            gp[rr, U] = (grad_hidden * silu).astype(BF)
        loop(PR // step, body)
        send(("py", j), gp.at[mine], gp.at[mine], YH)
        send(("pr0", j), gp.at[mine], gp.at[mine], RIGHT)
        send(("pl0", j), gp.at[mine], gp.at[mine], LEFT)
        send(("hr", j), hid.at[mine], hid.at[mine], RIGHT)
        send(("hl", j), hid.at[mine], hid.at[mine], LEFT)
        send(("hy0", j), hid.at[mine], hid.at[mine], YH)

    def a1(j):
        got(("py", j))
        other = rows_p(j, x, oh)
        send(("pr1", j), gp.at[other], gp.at[other], RIGHT)
        send(("pl1", j), gp.at[other], gp.at[other], LEFT)
        got(("pr0", j), ("pl0", j))
        fl, fr = rows_p(j, xl, h), rows_p(j, xr, h)
        send(("pfr0", j), gp.at[fl, G], gp.at[fl, G], RIGHT)
        send(("pfl0", j), gp.at[fr, U], gp.at[fr, U], LEFT)
        got(("hr", j), ("hl", j))
        send(("hfr", j), hid.at[fl, A], hid.at[fl, A], RIGHT)
        send(("hfl", j), hid.at[fr, B], hid.at[fr, B], LEFT)
        send(("hyl", j), hid.at[fl], hid.at[fl], YH)
        send(("hyr", j), hid.at[fr], hid.at[fr], YH)

    def a2(j):
        got(("pr1", j), ("pl1", j))
        fl, fr = rows_p(j, xl, oh), rows_p(j, xr, oh)
        send(("pfr1", j), gp.at[fl, G], gp.at[fl, G], RIGHT)
        send(("pfl1", j), gp.at[fr, U], gp.at[fr, U], LEFT)
        got(("hfr", j), ("hfl", j))
        ff = rows_p(j, xf, h)
        send(("hyf", j), hid.at[ff], hid.at[ff], YH)

    def d0(j):
        got(("pfr0", j), ("pfl0", j), ("pfr1", j), ("pfl1", j))
        got(("hy0", j), ("hyl", j), ("hyr", j), ("hyf", j))
        p0, p1 = DONE[j], DONE[j + 1]
        np_ = p1 - p0
        rows = pl.ds(p0 * 96, np_ * 96)

        def body(n):
            cs = pl.ds(pl.multiple_of(n * 256, 256), 256)
            er = pl.ds(pl.multiple_of((n // 2) * OWN, OWN), OWN)
            ec = pl.ds(pl.multiple_of((n % 2) * 256, 256), 256)
            for a in range(2):
                if a == 0:
                    v = dot_nn(hid[rows, :], wd[:, cs])
                else:
                    v = dot_nt(gp[rows, :], wcat[cs, :])
                v = v.reshape(np_, 2, 2, OWN, 256)
                for p in range(np_):
                    for dl in range(2):
                        e_own[a, dl, p0 + p, er, ec] = v[p, dl, 0]
                        e_sib[a, dl, p0 + p, er, ec] = v[p, dl, 1]
        loop(4, body)
        for dl in (1, 0):
            for a in range(2):
                for p in range(p0, p1):
                    e_sb[a, dl, p] = e_sib[a, dl, p].astype(BF)
                ps = pl.ds(p0, np_)
                send(("es", j, a, dl), e_sb.at[a, dl, ps], e_sr.at[a, dl, ps], SIB)

    def e2(j):
        p0, p1 = DONE[j], DONE[j + 1]
        ps = pl.ds(p0, p1 - p0)
        for a in range(2):
            got(("es", j, a, 1))
            for p in range(p0, p1):
                ey_s[a, p] = (e_own[a, 1, p] + e_sr[a, 1, p].astype(F32)).astype(BF)
            send(("ey", j, a), ey_s.at[a, ps], ey_r.at[a, ps], YL)

    def e3(j):
        p0, p1 = DONE[j], DONE[j + 1]
        for a in range(2):
            got(("es", j, a, 0), ("ey", j, a))
            for p in range(p0, p1):
                v = e_own[a, 0, p] + e_sr[a, 0, p].astype(F32) + ey_r[a, p].astype(F32)
                if DZ[p] == 0:
                    e_own[a, 0, p] = v
                else:
                    ez_s[a, p] = v.astype(BF)
                    send(("ez", p, a), ez_s.at[a, p], ez_r.at[a, p], ZL(DZ[p], 0))

    for q in range(NEED[0]):
        share(q)
    stages = [part, r1, r2, r3, a1, a2, d0, e2, e3]
    for t in range(NCH + len(stages) - 1):
        for k in reversed(range(len(stages))):
            j = t - k
            if 0 <= j < NCH:
                if k == 0:
                    if j + 1 < NCH:
                        for q in range(NEED[j], NEED[j + 1]):
                            share(q)
                    for q in range(NEED[j - 1] if j else 0, NEED[j]):
                        assemble(q)
                stages[k](j)

    scale = 1.0 / math.sqrt(TOK)

    def grads(i):
        cs = pl.ds(pl.multiple_of(i * 128, 128), 128)
        v = dot_tn(tok[:, cs], gp[...]) * scale
        for k in range(7):
            ks = pl.ds(k * 128, 128)
            gg_out[cs, ks] = (v[:, k * 128:(k + 1) * 128] * gm[i, k].astype(F32)).astype(BF)
            gu_out[cs, ks] = (v[:, FH + k * 128:FH + (k + 1) * 128] * um[i, k].astype(F32)).astype(BF)
    loop(8, grads)

    def gradd(i):
        cs = pl.ds(pl.multiple_of(i * 128, 128), 128)
        v = dot_tn(hid[:, cs], cot[...]) * scale
        for k in range(8):
            ks = pl.ds(k * 128, 128)
            gd_out[cs, ks] = (v[:, k * 128:(k + 1) * 128] * dm[i, k].astype(F32)).astype(BF)
    loop(7, gradd)

    for a, out in ((0, mix_out), (1, gt_out)):
        v = e_own[a, 0, SELF]
        for p in range(8):
            if p != SELF:
                got(("ez", p, a))
                v = v + ez_r[a, p].astype(F32)
        out[...] = jnp.concatenate([v[:OWN], v[OWN:]], axis=1).astype(BF)
    for d in sent.values():
        d.wait_send()


def on_device(tokens, gate_weight, up_weight, down_weight, gate_mask, up_mask, down_mask, grad_out):
    vm = pl.BlockSpec(memory_space=pltpu.VMEM)
    sm = pl.BlockSpec(memory_space=pltpu.SMEM)
    hbm = pl.BlockSpec(memory_space=pl.ANY)
    n_msg = 15 + 8 + NCH * (4 + 1 + 6 + 3 + 6 + 8 + 3 + 4 + 2) + 14
    V = pltpu.VMEM
    scratch = [
        V((W, 2 * FH), BF), V((FH, W), BF), V((2, OWN, W), BF),
        V((8, 2, 2, CH, 512), BF), V((8, 2, 2, CH, 512), BF), V((TOK, W), BF), V((TOK, W), BF),
        V((TOK, 2 * FH), BF), V((NCH, 4, 2, PR, FH), BF),
        V((NCH, XR, FH), BF), V((NCH, XR, FH), BF),
        V((NCH, 2, XR, FH), BF), V((NCH, 2, XR, FH), BF),
        V((NCH, PR, 2 * FH), F32), V((NCH, PR, 2 * FH), BF), V((NCH, PR, 2 * FH), BF),
        V((NCH, 4, PR, FH), BF), V((NCH, PR, CA), BF), V((NCH, PR, FH - CA), BF), V((NCH, 2, PR, FH), BF),
        V((TOK, FH), BF), V((TOK, 2 * FH), BF),
        V((2, 2, 8, CH, 512), F32), V((2, 2, 8, CH, 512), F32),
        V((2, 2, 8, CH, 512), BF), V((2, 2, 8, CH, 512), BF),
        V((2, 8, CH, 512), BF), V((2, 8, CH, 512), BF), V((2, 8, CH, 512), BF), V((2, 8, CH, 512), BF),
        pltpu.SemaphoreType.DMA((5,)), pltpu.SemaphoreType.DMA((n_msg,)), pltpu.SemaphoreType.DMA((n_msg,)),
    ]
    return pl.pallas_call(
        kernel,
        out_shape=(
            jax.ShapeDtypeStruct((OWN, W), BF),
            jax.ShapeDtypeStruct((OWN, W), BF),
            jax.ShapeDtypeStruct((W, FH), BF),
            jax.ShapeDtypeStruct((W, FH), BF),
            jax.ShapeDtypeStruct((FH, W), BF),
        ),
        in_specs=[hbm, hbm, hbm, hbm, sm, sm, sm, hbm],
        out_specs=(vm, vm, vm, vm, vm),
        scratch_shapes=scratch,
        name="layer",
        compiler_params=pltpu.CompilerParams(
            collective_id=0, has_side_effects=True, vmem_limit_bytes=60 << 20
        ),
        cost_estimate=pl.CostEstimate(flops=9 * 2 * TOK * W * FH, bytes_accessed=12 << 20, transcendentals=TOK * FH),
    )(tokens, gate_weight, up_weight, down_weight, gate_mask, up_mask, down_mask, grad_out)


def solution(mesh):
    placed = (
        P("mp", "seq"),
        P("seq", "mp"),
        P("seq", "mp"),
        P("mp", "seq"),
        P("seq", "mp"),
        P("seq", "mp"),
        P("mp", "seq"),
        P("mp", "seq"),
    )
    return jax.shard_map(
        on_device,
        mesh=mesh,
        in_specs=placed,
        out_specs=(P("mp", "seq"), P("mp", "seq"), P("seq", "mp"), P("seq", "mp"), P("mp", "seq")),
        check_vma=False,
    )
```

```python
import math

import jax
import jax.numpy as jnp
from jax import lax
from jax.experimental import pallas as pl
from jax.experimental.pallas import tpu as pltpu
from jax.sharding import PartitionSpec as P

MESH = pl.DeviceIdType.MESH
BF = jnp.bfloat16
F32 = jnp.float32

TOK = 768
W = 1024
FH = 896
OWN = 24
CH = 48
CA = 512
CS = (128, 256, 256, 128)
DZ = (0, 1, 7, 2, 4, 5, 3, 6)
YFIRST = (False, False, True, True)
ORDER = (
    ("ag", 0), ("mgu",), ("ag", 1), ("md",), ("agy", 0), ("agy", 1), ("asm", 0, 0), ("agz", 0, 1), ("asm", 1, 0),
    ("agz", 1, 1), ("asm", 0, 2), ("asm", 0, 1), ("gu", 0), ("asm", 1, 2), ("asm", 1, 1), ("hd", 0), ("agz", 0, 2),
    ("gu1", 0), ("agz", 1, 2), ("asm", 0, 3), ("gu", 1), ("asm", 0, 7), ("asm", 1, 7), ("agz", 0, 3), ("asm", 1, 3),
    ("hd1", 0), ("gu2", 0), ("asm", 0, 5), ("agz", 1, 3), ("hd", 1), ("asm", 0, 6), ("agz", 0, 4), ("gu1", 1),
    ("asm", 1, 5), ("asm", 1, 6), ("asm", 0, 4), ("agz", 1, 4), ("act", 0), ("gu", 2), ("hd2", 0), ("asm", 1, 4),
    ("gu2", 1), ("hx", 0), ("hd1", 1), ("hd", 2), ("gu1", 2), ("act2", 0), ("act", 1), ("hf", 0), ("hd2", 1),
    ("gu", 3), ("gu2", 2), ("pf", 0, 0), ("hd1", 2), ("hd", 3), ("act2", 1), ("hx", 1), ("py", 0), ("gu1", 3),
    ("d", 0, 0), ("hd2", 2), ("ea", 0, 0), ("act", 2), ("pf", 1, 0), ("hd1", 3), ("hf", 1), ("pf", 0, 1), ("py", 1),
    ("gu2", 3), ("act2", 2), ("hx", 2), ("hd2", 3), ("d", 1, 0), ("d", 0, 1), ("act", 3), ("ea", 1, 0), ("pf", 1, 1),
    ("py", 2), ("ea", 0, 1), ("pf", 2, 0), ("hf", 2), ("act2", 3), ("hx", 3), ("d", 1, 1), ("d", 0, 2), ("pf", 2, 1),
    ("py", 3), ("ea", 1, 1), ("ea", 0, 2), ("pf", 3, 0), ("hf", 3), ("d", 1, 2), ("pf", 3, 1), ("ea", 1, 2),
    ("d", 0, 3), ("eb", 0, 2), ("d", 1, 3), ("ea", 0, 3), ("wd",), ("eb", 1, 2), ("ea", 1, 3), ("wgp",), ("eb", 0, 3),
    ("f1", 0), ("eb", 1, 3), ("f1", 1), ("f2", 0), ("f2", 1),
)

NCH = len(CS)
OFF = [sum(CS[:j]) for j in range(NCH + 1)]
NEG = tuple(DZ.index((8 - d) % 8) for d in DZ)
SELF = DZ.index(0)
DONE = [o // 96 for o in OFF]


def dot_nn(a, b):
    return jnp.dot(a, b, preferred_element_type=F32)


def dot_nt(a, b):
    return lax.dot_general(a, b, (((1,), (1,)), ((), ())), preferred_element_type=F32)


def dot_tn(a, b):
    return lax.dot_general(a, b, (((0,), (0,)), ((), ())), preferred_element_type=F32)


def loop(n, body):
    for i in range(n):
        body(i)


def buffers():
    V = pltpu.VMEM
    b = dict(
        wcat=V((W, 2 * FH), BF), wd=V((FH, W), BF), io_buf=V((2, OWN, W), BF),
        slot_o=V((2, 8, 2, CH, 512), BF), slot_s=V((2, 8, 2, CH, 512), BF),
        tok=V((TOK, W), BF), cot=V((TOK, W), BF),
        p_gu=V((TOK, 2 * FH), BF), hid=V((TOK, FH), BF), gp=V((TOK, 2 * FH), BF),
        e_own=V((2, 2, 8, CH, 512), F32), e_sib=V((2, 2, 8, CH, 512), F32),
        e_sb=V((2, 2, 8, CH, 512), BF), e_sr=V((2, 2, 8, CH, 512), BF),
        ey_s=V((2, 8, CH, 512), BF), ey_r=V((2, 8, CH, 512), BF),
        ez_s=V((2, 8, 2, CH, 512), BF), ez_r=V((2, 8, 2, CH, 512), BF),
        ef_s=V((2, CH, 512), BF), ef_r=V((2, CH, 512), BF),
        gg_b=V((W, FH), BF), gu_b=V((W, FH), BF), gd_b=V((FH, W), BF),
    )
    for j, r in enumerate(CS):
        pr, xr = r // 8, r // 4
        b.update({
            ("p_h", j): V((4, 2, pr, FH), BF), ("fy_h", j): V((4, pr, FH), BF),
            ("f1g", j): V((xr, FH), BF), ("f1u", j): V((xr, FH), BF),
            ("f2g", j): V((2, xr, FH), BF), ("f2u", j): V((2, xr, FH), BF),
            ("own_gu", j): V((pr, 2 * FH), F32), ("sy_gu", j): V((pr, 2 * FH), BF),
            ("fy_gu", j): V((pr, 2 * FH), BF),
            ("f1a", j): V((pr, CA), BF), ("f1b", j): V((pr, FH - CA), BF),
            ("f2h", j): V((2, pr, FH), BF),
        })
    return b


def kernel(*refs):
    (tok_in, gw_in, uw_in, dw_in, gm, um, dm, cot_in, mix_out, gt_out, gg_out, gu_out, gd_out) = refs[:13]
    b = dict(zip(buffers(), refs[13:-3]))
    lsem, ssem, rsem = refs[-3:]
    wcat, wd, io_buf, slot_o, slot_s = (b[k] for k in ("wcat", "wd", "io_buf", "slot_o", "slot_s"))
    tok, cot, p_gu, hid, gp = (b[k] for k in ("tok", "cot", "p_gu", "hid", "gp"))
    e_own, e_sib, e_sb, e_sr = (b[k] for k in ("e_own", "e_sib", "e_sb", "e_sr"))

    s = lax.axis_index("seq")
    m = lax.axis_index("mp")
    h, x = s // 4, s % 4
    l, z, c = m // 16, (m // 2) % 8, m % 2
    xr, xl, xf = (x + 1) % 4, (x + 3) % 4, (x + 2) % 4
    oh = 1 - h

    def mp_of(dz, dl, dc=0):
        return ((l + dl) % 2) * 16 + ((z + dz) % 8) * 2 + (c + dc) % 2

    RIGHT, LEFT, YH = (h * 4 + xr, m), (h * 4 + xl, m), (oh * 4 + x, m)
    SIB, YL = (s, mp_of(0, 0, 1)), (s, mp_of(0, 1))

    def ZL(dz):
        return (s, mp_of(dz, 0))

    sent, waited = {}, set()

    def send(key, src, dst, to):
        k = len(sent)
        d = pltpu.make_async_remote_copy(
            src_ref=src, dst_ref=dst, send_sem=ssem.at[k], recv_sem=rsem.at[k],
            device_id=to, device_id_type=MESH,
        )
        d.start()
        sent[key] = d

    def got(*keys):
        for key in keys:
            if key not in waited:
                waited.add(key)
                sent[key].wait_recv()

    loads = [
        pltpu.make_async_copy(tok_in, io_buf.at[0], lsem.at[0]),
        pltpu.make_async_copy(cot_in, io_buf.at[1], lsem.at[1]),
        pltpu.make_async_copy(gw_in, wcat.at[:, pl.ds(0, FH)], lsem.at[2]),
        pltpu.make_async_copy(uw_in, wcat.at[:, pl.ds(FH, FH)], lsem.at[3]),
        pltpu.make_async_copy(dw_in, wd, lsem.at[4]),
    ]
    for d in loads:
        d.start()
    stores = []

    barrier = pltpu.get_barrier_semaphore()
    peers = [RIGHT, LEFT, YH, SIB, YL] + [ZL(dz) for dz in range(1, 8)]
    for to in peers:
        pl.semaphore_signal(barrier, inc=1, device_id=to, device_id_type=MESH)

    def pack(v):
        v = v.astype(F32)
        return jnp.concatenate([v[:, :512], v[:, 512:]], axis=0).astype(BF)

    def unpack(v):
        v = v.astype(F32)
        return jnp.concatenate([v[:OWN], v[OWN:]], axis=1)

    for a in range(2):
        loads[a].wait()
        slot_o[a, SELF, 0] = pack(io_buf[a])
    pl.semaphore_wait(barrier, len(peers))

    def at(dz):
        return DZ.index(dz % 8)

    def hop_r(a, d, dl):
        send(("r", a, d, dl), slot_o.at[a, at(1 - d), dl], slot_o.at[a, at(-d), dl], ZL(1))

    def hop_l(a, d, dl):
        send(("l", a, d, dl), slot_o.at[a, at(d - 1), dl], slot_o.at[a, at(d), dl], ZL(7))

    def t_ag(a):
        send(("yl", a), slot_o.at[a, SELF, 0], slot_o.at[a, SELF, 1], YL)
        hop_r(a, 1, 0)
        hop_l(a, 1, 0)

    def t_agy(a):
        got(("yl", a))
        hop_r(a, 1, 1)
        hop_l(a, 1, 1)
        send(("sh", a, SELF), slot_o.at[a, SELF], slot_s.at[a, SELF], SIB)

    def t_agz(a, d):
        for dl in range(2):
            if d < 4 or dl == 0:
                got(("r", a, d, dl))
            if d < 3 or (d == 3 and dl == 0):
                hop_r(a, d + 1, dl)
            if d < 4 or dl == 1:
                got(("l", a, d, dl))
            if d < 3 or (d == 3 and dl == 1):
                hop_l(a, d + 1, dl)
        for q in (at(-d), at(d))[: 2 if d < 4 else 1]:
            send(("sh", a, q), slot_o.at[a, q], slot_s.at[a, q], SIB)

    def t_asm(a, q):
        got(("sh", a, q))
        ref = (tok, cot)[a]
        for dl in range(2):
            v = jnp.concatenate([unpack(slot_o[a, q, dl]), unpack(slot_s[a, q, dl])], axis=0)
            ref[pl.ds(q * 96 + dl * CH, CH), :] = v.astype(BF)

    def masked(ref, mask, rows, cols, col0):
        def body(i):
            r = pl.ds(i * 128, 128)
            for k in range(cols):
                cs = pl.ds(col0 + k * 128, 128)
                ref[r, cs] = (ref[r, cs].astype(F32) * mask[i, k].astype(F32)).astype(BF)
        loop(rows, body)

    def t_mgu():
        loads[2].wait()
        masked(wcat, gm, 8, 7, 0)
        loads[3].wait()
        masked(wcat, um, 8, 7, FH)

    def t_md():
        loads[4].wait()
        masked(wd, dm, 7, 8, 0)

    def rows_x(j, xi):
        return pl.ds(pl.multiple_of(OFF[j] + xi * (CS[j] // 4), CS[j] // 4), CS[j] // 4)

    def rows_p(j, xi, hi):
        return pl.ds(pl.multiple_of(OFF[j] + xi * (CS[j] // 4) + hi * (CS[j] // 8), CS[j] // 8), CS[j] // 8)

    G, U = pl.ds(0, FH), pl.ds(FH, FH)
    A, B = pl.ds(0, CA), pl.ds(CA, FH - CA)

    def t_gu(j):
        rows = pl.ds(OFF[j], CS[j])

        def body(n):
            cs = pl.ds(n * 256, 256)
            p_gu[rows, cs] = dot_nn(tok[rows, :], wcat[:, cs]).astype(BF)
        loop(7, body)
        send(("g1", j), p_gu.at[rows_x(j, xf), G], b["f1g", j], RIGHT)
        send(("u1", j), p_gu.at[rows_x(j, xf), U], b["f1u", j], LEFT)
        send(("g2l", j), p_gu.at[rows_x(j, xl), G], b["f2g", j].at[1], LEFT)
        send(("u2r", j), p_gu.at[rows_x(j, xr), U], b["f2u", j].at[0], RIGHT)

    def t_hd(j):
        rows, p_h, pr = pl.ds(OFF[j], CS[j]), b["p_h", j], CS[j] // 8

        def body(n):
            cs = pl.ds(n * 256, 256)
            p_h[:, :, :, cs] = dot_nt(cot[rows, :], wd[cs, :]).astype(BF).reshape(4, 2, pr, 256)
        loop(3, body)
        cs = pl.ds(768, 128)
        p_h[:, :, :, cs] = dot_nt(cot[rows, :], wd[cs, :]).astype(BF).reshape(4, 2, pr, 128)
        send(("hy", j), p_h.at[:, oh], b["fy_h", j], YH)

    def add_to(ref, at_, other):
        ref[at_] = (ref[at_].astype(F32) + other[...].astype(F32)).astype(BF)

    def t_gu1(j):
        got(("g1", j))
        rows = rows_x(j, xr)
        add_to(p_gu, (rows, G), b["f1g", j])
        send(("g2r", j), p_gu.at[rows, G], b["f2g", j].at[0], RIGHT)
        got(("u1", j))
        rows = rows_x(j, xl)
        add_to(p_gu, (rows, U), b["f1u", j])
        send(("u2l", j), p_gu.at[rows, U], b["f2u", j].at[1], LEFT)

    def t_hd1(j):
        p_h, f2h = b["p_h", j], b["f2h", j]
        got(("hy", j))
        for xi in range(4):
            add_to(p_h, (xi, h), b["fy_h", j].at[xi])
        send(("h1a", j), p_h.at[xf, h, :, A], b["f1a", j], RIGHT)
        send(("h1b", j), p_h.at[xf, h, :, B], b["f1b", j], LEFT)
        send(("h2rb", j), p_h.at[xr, h, :, B], f2h.at[0, :, B], RIGHT)
        send(("h2la", j), p_h.at[xl, h, :, A], f2h.at[1, :, A], LEFT)

    def t_hd2(j):
        p_h, f2h = b["p_h", j], b["f2h", j]
        got(("h1a", j))
        add_to(p_h, (xr, h, slice(None), A), b["f1a", j])
        send(("h2ra", j), p_h.at[xr, h, :, A], f2h.at[0, :, A], RIGHT)
        got(("h1b", j))
        add_to(p_h, (xl, h, slice(None), B), b["f1b", j])
        send(("h2lb", j), p_h.at[xl, h, :, B], f2h.at[1, :, B], LEFT)

    def t_gu2(j):
        pr = CS[j] // 8
        got(("g2l", j), ("u2r", j), ("g2r", j), ("u2l", j))
        for f2, cs in ((b["f2g", j], G), (b["f2u", j], U)):
            def total(hi):
                r = pl.ds(pl.multiple_of(hi * pr, pr), pr)
                return p_gu[rows_p(j, x, hi), cs].astype(F32) + f2[0, r, :].astype(F32) + f2[1, r, :].astype(F32)
            b["sy_gu", j][:, cs] = total(oh).astype(BF)
            b["own_gu", j][:, cs] = total(h)
        send(("guy", j), b["sy_gu", j], b["fy_gu", j], YH)

    def steps(j, body):
        def at_(i):
            r = pl.ds(i * 16, 16)
            rr = pl.ds(pl.multiple_of(OFF[j] + x * (CS[j] // 4) + h * (CS[j] // 8) + i * 16, 16), 16)
            body(r, rr)
        loop(CS[j] // 128, at_)

    def t_act(j):
        got(("guy", j))
        own_gu, fy_gu = b["own_gu", j], b["fy_gu", j]

        def body(r, rr):
            pre_gate = own_gu[r, G] + fy_gu[r, G].astype(F32)
            pre_up = own_gu[r, U] + fy_gu[r, U].astype(F32)
            own_gu[r, G] = pre_gate
            own_gu[r, U] = pre_up
            hid[rr, :] = (pre_gate * jax.nn.sigmoid(pre_gate) * pre_up).astype(BF)
        steps(j, body)
        mine = rows_p(j, x, h)
        send(("hr", j), hid.at[mine], hid.at[mine], RIGHT)
        send(("hl", j), hid.at[mine], hid.at[mine], LEFT)
        send(("hy0", j), hid.at[mine], hid.at[mine], YH)

    def t_act2(j):
        got(("h2rb", j), ("h2la", j), ("h2ra", j), ("h2lb", j))
        own_gu, p_h, f2h = b["own_gu", j], b["p_h", j], b["f2h", j]

        def body(r, rr):
            pre_gate, pre_up = own_gu[r, G], own_gu[r, U]
            grad_hidden = p_h[x, h, r, :].astype(F32) + f2h[0, r, :].astype(F32) + f2h[1, r, :].astype(F32)
            sig = jax.nn.sigmoid(pre_gate)
            gp[rr, G] = (grad_hidden * pre_up * sig * (1.0 + pre_gate * (1.0 - sig))).astype(BF)
            gp[rr, U] = (grad_hidden * (pre_gate * sig)).astype(BF)
        steps(j, body)
        mine = rows_p(j, x, h)
        send(("py", j), gp.at[mine], gp.at[mine], YH)
        send(("pr0", j), gp.at[mine], gp.at[mine], RIGHT)
        send(("pl0", j), gp.at[mine], gp.at[mine], LEFT)

    def t_hx(j):
        fl, fr = rows_p(j, xl, h), rows_p(j, xr, h)
        got(("hr", j))
        send(("hfr", j), hid.at[fl, A], hid.at[fl, A], RIGHT)
        got(("hl", j))
        send(("hfl", j), hid.at[fr, B], hid.at[fr, B], LEFT)
        send(("hyl", j), hid.at[fl], hid.at[fl], YH)
        send(("hyr", j), hid.at[fr], hid.at[fr], YH)

    def t_hf(j):
        got(("hfr", j), ("hfl", j))
        ff = rows_p(j, xf, h)
        send(("hyf", j), hid.at[ff], hid.at[ff], YH)

    def t_py(j):
        got(("py", j))
        other = rows_p(j, x, oh)
        send(("pr1", j), gp.at[other], gp.at[other], RIGHT)
        send(("pl1", j), gp.at[other], gp.at[other], LEFT)

    def t_pf(j, k):
        fl, fr = rows_p(j, xl, (h, oh)[k]), rows_p(j, xr, (h, oh)[k])
        got((("pr0", "pr1")[k], j))
        send(("pfr", j, k), gp.at[fl, G], gp.at[fl, G], RIGHT)
        got((("pl0", "pl1")[k], j))
        send(("pfl", j, k), gp.at[fr, U], gp.at[fr, U], LEFT)

    def t_d(a, j):
        if a == 0:
            got(("hy0", j), ("hyl", j), ("hyr", j), ("hyf", j))
        else:
            got(("pfr", j, 0), ("pfl", j, 0), ("pfr", j, 1), ("pfl", j, 1))
        p0, p1 = DONE[j], DONE[j + 1]
        n_p = p1 - p0
        rows = pl.ds(p0 * 96, n_p * 96)

        def body(n):
            cs = pl.ds(n * 256, 256)
            er = pl.ds((n // 2) * OWN, OWN)
            ec = pl.ds((n % 2) * 256, 256)
            v = dot_nn(hid[rows, :], wd[:, cs]) if a == 0 else dot_nt(gp[rows, :], wcat[cs, :])
            v = v.reshape(n_p, 2, 2, OWN, 256)
            for p in range(n_p):
                for dl in range(2):
                    e_own[a, dl, p0 + p, er, ec] = v[p, dl, 0]
                    e_sib[a, dl, p0 + p, er, ec] = v[p, dl, 1]
        loop(4, body)
        for dl in (1, 0):
            for p in range(p0, p1):
                e_sb[a, dl, p] = e_sib[a, dl, p].astype(BF)
            ps = pl.ds(p0, n_p)
            send(("es", a, j, dl), e_sb.at[a, dl, ps], e_sr.at[a, dl, ps], SIB)

    def to_z(a, p, dl, v):
        if p == SELF:
            e_own[a, dl, p] = v
        else:
            b["ez_s"][a, p, dl] = v.astype(BF)
            send(("ez", a, p, dl), b["ez_s"].at[a, p, dl], b["ez_r"].at[a, p, dl], ZL(DZ[p]))

    def t_ea(a, j):
        p0, p1 = DONE[j], DONE[j + 1]
        if YFIRST[j]:
            got(("es", a, j, 1))
            for p in range(p0, p1):
                b["ey_s"][a, p] = (e_own[a, 1, p] + e_sr[a, 1, p].astype(F32)).astype(BF)
            ps = pl.ds(p0, p1 - p0)
            send(("ey", a, j), b["ey_s"].at[a, ps], b["ey_r"].at[a, ps], YL)
        else:
            for dl in (1, 0):
                got(("es", a, j, dl))
                for p in range(p0, p1):
                    to_z(a, p, dl, e_own[a, dl, p] + e_sr[a, dl, p].astype(F32))

    def t_eb(a, j):
        got(("es", a, j, 0), ("ey", a, j))
        for p in range(DONE[j], DONE[j + 1]):
            to_z(a, p, 0, e_own[a, 0, p] + e_sr[a, 0, p].astype(F32) + b["ey_r"][a, p].astype(F32))

    ZF = [p for j in range(NCH) for p in range(DONE[j], DONE[j + 1]) if not YFIRST[j]]

    def whole(a, dl, pairs):
        v = e_own[a, dl, SELF] if SELF in pairs else None
        for p in pairs:
            if p != SELF:
                got(("ez", a, p, dl))
                t = b["ez_r"][a, p, dl].astype(F32)
                v = t if v is None else v + t
        return v

    def t_f1(a):
        b["ef_s"][a] = whole(a, 1, ZF).astype(BF)
        send(("ef", a), b["ef_s"].at[a], b["ef_r"].at[a], YL)

    def t_f2(a):
        v = whole(a, 0, range(8))
        if ZF:
            got(("ef", a))
            v = v + b["ef_r"][a].astype(F32)
        (mix_out, gt_out)[a][...] = jnp.concatenate([v[:OWN], v[OWN:]], axis=1).astype(BF)

    scale = 1.0 / math.sqrt(TOK)

    def store(k, src, dst):
        d = pltpu.make_async_copy(src, dst, lsem.at[k])
        d.start()
        stores.append(d)

    def t_wgp():
        def body(i):
            cs = pl.ds(i * 128, 128)
            v = dot_tn(tok[:, cs], gp[...]) * scale
            for k in range(7):
                ks = pl.ds(k * 128, 128)
                b["gg_b"][cs, ks] = (v[:, k * 128:(k + 1) * 128] * gm[i, k].astype(F32)).astype(BF)
                b["gu_b"][cs, ks] = (v[:, FH + k * 128:FH + (k + 1) * 128] * um[i, k].astype(F32)).astype(BF)
        loop(8, body)
        store(0, b["gg_b"], gg_out)
        store(1, b["gu_b"], gu_out)

    def t_wd():
        def body(i):
            cs = pl.ds(i * 128, 128)
            v = dot_tn(hid[:, cs], cot[...]) * scale
            for k in range(8):
                ks = pl.ds(k * 128, 128)
                b["gd_b"][cs, ks] = (v[:, k * 128:(k + 1) * 128] * dm[i, k].astype(F32)).astype(BF)
        loop(7, body)
        store(2, b["gd_b"], gd_out)

    do = dict(
        ag=t_ag, agy=t_agy, agz=t_agz, asm=t_asm, mgu=t_mgu, md=t_md, gu=t_gu, hd=t_hd, gu1=t_gu1, hd1=t_hd1, hd2=t_hd2,
        gu2=t_gu2, act=t_act, act2=t_act2, hx=t_hx, hf=t_hf, py=t_py, pf=t_pf, d=t_d, ea=t_ea, eb=t_eb, f1=t_f1, f2=t_f2,
        wgp=t_wgp, wd=t_wd,
    )
    for name, *which in ORDER:
        do[name](*which)
    for d in list(sent.values()):
        d.wait_send()
    for d in stores:
        d.wait()


def hand_on(*refs):
    ins, outs, held, (in_sem, out_sem) = refs[:5], refs[5:10], refs[10:15], refs[15:]
    reads, writes = [], []
    for k in (2, 3, 4, 0, 1):
        n = 4 if ins[k].shape[0] > OWN else 1
        for i in range(n):
            r = pl.ds(i * (ins[k].shape[0] // n), ins[k].shape[0] // n)
            t = len(reads)
            reads.append(pltpu.make_async_copy(ins[k].at[r], held[k].at[r], in_sem.at[t]))
            writes.append(pltpu.make_async_copy(held[k].at[r], outs[k].at[r], out_sem.at[t]))
            reads[t].start()
    for read, write in zip(reads, writes):
        read.wait()
        write.start()
    for write in writes:
        write.wait()


def on_device(tokens, gate_weight, up_weight, down_weight, gate_mask, up_mask, down_mask, grad_out):
    vm = pl.BlockSpec(memory_space=pltpu.VMEM)
    sm = pl.BlockSpec(memory_space=pltpu.SMEM)
    hbm = pl.BlockSpec(memory_space=pl.ANY)
    n_msg = 46 + NCH * 37 + 2 * 14 + 2
    D, V = pltpu.SemaphoreType.DMA, pltpu.VMEM
    outs = pl.pallas_call(
        kernel,
        out_shape=(
            jax.ShapeDtypeStruct((OWN, W), BF),
            jax.ShapeDtypeStruct((OWN, W), BF),
            jax.ShapeDtypeStruct((W, FH), BF),
            jax.ShapeDtypeStruct((W, FH), BF),
            jax.ShapeDtypeStruct((FH, W), BF),
        ),
        in_specs=[hbm, hbm, hbm, hbm, sm, sm, sm, hbm],
        out_specs=(vm, vm, hbm, hbm, hbm),
        scratch_shapes=[*buffers().values(), D((5,)), D((n_msg,)), D((n_msg,))],
        name="layer",
        compiler_params=pltpu.CompilerParams(
            collective_id=0, has_side_effects=True, vmem_limit_bytes=60 << 20
        ),
        cost_estimate=pl.CostEstimate(flops=9 * 2 * TOK * W * FH, bytes_accessed=12 << 20, transcendentals=TOK * FH),
    )(tokens, gate_weight, up_weight, down_weight, gate_mask, up_mask, down_mask, grad_out)
    return pl.pallas_call(
        hand_on,
        out_shape=tuple(jax.ShapeDtypeStruct(o.shape, o.dtype) for o in outs),
        in_specs=[hbm] * 5,
        out_specs=(hbm,) * 5,
        scratch_shapes=[V(o.shape, o.dtype) for o in outs] + [D((14,)), D((14,))],
        name="hand_on",
        compiler_params=pltpu.CompilerParams(vmem_limit_bytes=60 << 20),
        cost_estimate=pl.CostEstimate(flops=0, bytes_accessed=12 << 20, transcendentals=0),
    )(*outs)


def solution(mesh):
    placed = (
        P("mp", "seq"),
        P("seq", "mp"),
        P("seq", "mp"),
        P("mp", "seq"),
        P("seq", "mp"),
        P("seq", "mp"),
        P("mp", "seq"),
        P("mp", "seq"),
    )
    return jax.shard_map(
        on_device,
        mesh=mesh,
        in_specs=placed,
        out_specs=(P("mp", "seq"), P("mp", "seq"), P("seq", "mp"), P("seq", "mp"), P("mp", "seq")),
        check_vma=False,
    )
```

```python
import math

import jax
import jax.numpy as jnp
from jax import lax
from jax.experimental import pallas as pl
from jax.experimental.pallas import tpu as pltpu
from jax.sharding import PartitionSpec as P

MESH = pl.DeviceIdType.MESH
BF = jnp.bfloat16
F32 = jnp.float32

TOK = 768
W = 1024
FH = 896
OWN = 24
CH = 48
CA = 512
CS = (128, 256, 256, 128)
DZ = (1, 0, 7, 2, 4, 5, 3, 6)
YFIRST = (False, False, True, True)
ORDER = (
    ("ag", 0), ("md",), ("ag", 1), ("mgu",), ("agy", 0), ("agy", 1), ("agz", 0, 1), ("asm", 0, 1), ("agz", 1, 1),
    ("asm", 0, 0), ("gu", 0), ("asm", 1, 2), ("agz", 0, 2), ("asm", 1, 0), ("asm", 0, 2), ("asm", 1, 1), ("hd", 0),
    ("agz", 1, 2), ("gu1", 0), ("asm", 0, 3), ("gu", 1), ("asm", 1, 3), ("agz", 0, 3), ("hd", 1), ("agz", 1, 3),
    ("asm", 0, 6), ("hd1", 0), ("gu2", 0), ("asm", 1, 7), ("agz", 0, 4), ("gu1", 1), ("asm", 1, 6), ("asm", 0, 5),
    ("agz", 1, 4), ("asm", 0, 4), ("gu", 2), ("asm", 1, 5), ("asm", 1, 4), ("hd", 2), ("hd2", 0), ("hd1", 1),
    ("gu2", 1), ("gu1", 2), ("hd", 3), ("act", 0), ("act2", 0), ("asm", 0, 7), ("gu", 3), ("gu2", 2), ("hx", 0),
    ("act", 1), ("hd2", 1), ("hd1", 2), ("gu1", 3), ("hf", 0), ("hx", 1), ("hd1", 3), ("hd2", 2), ("act2", 1),
    ("hf", 1), ("act", 2), ("py", 0), ("gu2", 3), ("d", 0, 0), ("act2", 2), ("hx", 2), ("py", 1), ("pf", 0, 1),
    ("d", 0, 1), ("hd2", 3), ("ea", 0, 0), ("hf", 2), ("pf", 0, 0), ("act", 3), ("pf", 1, 0), ("pf", 1, 1),
    ("ea", 0, 1), ("py", 2), ("d", 1, 0), ("hx", 3), ("act2", 3), ("pf", 2, 0), ("d", 0, 2), ("d", 1, 1),
    ("pf", 2, 1), ("ea", 1, 0), ("ea", 0, 2), ("pf", 3, 0), ("py", 3), ("hf", 3), ("ea", 1, 1), ("d", 1, 2),
    ("pf", 3, 1), ("eb", 0, 2), ("ea", 1, 2), ("d", 0, 3), ("d", 1, 3), ("ea", 0, 3), ("eb", 1, 2), ("wgp", 3),
    ("ea", 1, 3), ("eb", 0, 3), ("wd", 0), ("eb", 1, 3), ("f1", 1), ("wd", 1), ("f1", 0), ("wgp", 2), ("wd", 3),
    ("wgp", 0), ("wd", 2), ("f2", 0), ("wgp", 1), ("f2", 1),
)

NCH = len(CS)
OFF = [sum(CS[:j]) for j in range(NCH + 1)]
NEG = tuple(DZ.index((8 - d) % 8) for d in DZ)
SELF = DZ.index(0)
DONE = [o // 96 for o in OFF]


def dot_nn(a, b):
    return jnp.dot(a, b, preferred_element_type=F32)


def dot_nt(a, b):
    return lax.dot_general(a, b, (((1,), (1,)), ((), ())), preferred_element_type=F32)


def dot_tn(a, b):
    return lax.dot_general(a, b, (((0,), (0,)), ((), ())), preferred_element_type=F32)


def loop(n, body):
    for i in range(n):
        body(i)


def buffers():
    V = pltpu.VMEM
    b = dict(
        wcat=V((W, 2 * FH), BF), wd=V((FH, W), BF), io_buf=V((2, OWN, W), BF),
        slot_o=V((2, 8, 2, CH, 512), BF), slot_s=V((2, 8, 2, CH, 512), BF),
        tok=V((TOK, W), BF), cot=V((TOK, W), BF),
        p_gu=V((TOK, 2 * FH), BF), hid=V((TOK, FH), BF), gp=V((TOK, 2 * FH), BF),
        e_own=V((2, 2, 8, CH, 512), F32), e_sib=V((2, 2, 8, CH, 512), F32),
        e_sb=V((2, 2, 8, CH, 512), BF), e_sr=V((2, 2, 8, CH, 512), BF),
        ey_s=V((2, 8, CH, 512), BF), ey_r=V((2, 8, CH, 512), BF),
        ez_s=V((2, 8, 2, CH, 512), BF), ez_r=V((2, 8, 2, CH, 512), BF),
        ef_s=V((2, CH, 512), BF), ef_r=V((2, CH, 512), BF),
        gg_b=V((W, FH), BF), gu_b=V((W, FH), BF), gd_b=V((FH, W), BF),
    )
    for j, r in enumerate(CS):
        pr, xr = r // 8, r // 4
        b.update({
            ("p_h", j): V((4, 2, pr, FH), BF), ("fy_h", j): V((4, pr, FH), BF),
            ("f1g", j): V((xr, FH), BF), ("f1u", j): V((xr, FH), BF),
            ("f2g", j): V((2, xr, FH), BF), ("f2u", j): V((2, xr, FH), BF),
            ("own_gu", j): V((pr, 2 * FH), F32), ("sy_gu", j): V((pr, 2 * FH), BF),
            ("fy_gu", j): V((pr, 2 * FH), BF),
            ("f1a", j): V((pr, CA), BF), ("f1b", j): V((pr, FH - CA), BF),
            ("f2h", j): V((2, pr, FH), BF),
        })
    return b


def kernel(*refs):
    (tok_in, gw_in, uw_in, dw_in, gm, um, dm, cot_in, mix_out, gt_out, gg_out, gu_out, gd_out) = refs[:13]
    b = dict(zip(buffers(), refs[13:-3]))
    lsem, ssem, rsem = refs[-3:]
    wcat, wd, io_buf, slot_o, slot_s = (b[k] for k in ("wcat", "wd", "io_buf", "slot_o", "slot_s"))
    tok, cot, p_gu, hid, gp = (b[k] for k in ("tok", "cot", "p_gu", "hid", "gp"))
    e_own, e_sib, e_sb, e_sr = (b[k] for k in ("e_own", "e_sib", "e_sb", "e_sr"))

    s = lax.axis_index("seq")
    m = lax.axis_index("mp")
    h, x = s // 4, s % 4
    l, z, c = m // 16, (m // 2) % 8, m % 2
    xr, xl, xf = (x + 1) % 4, (x + 3) % 4, (x + 2) % 4
    oh = 1 - h

    def mp_of(dz, dl, dc=0):
        return ((l + dl) % 2) * 16 + ((z + dz) % 8) * 2 + (c + dc) % 2

    RIGHT, LEFT, YH = (h * 4 + xr, m), (h * 4 + xl, m), (oh * 4 + x, m)
    SIB, YL = (s, mp_of(0, 0, 1)), (s, mp_of(0, 1))

    def ZL(dz, dl=0):
        return (s, mp_of(dz, dl))

    sent, waited, leaving = {}, set(), []

    def send(key, src, dst, to):
        k = len(sent)
        d = pltpu.make_async_remote_copy(
            src_ref=src, dst_ref=dst, send_sem=ssem.at[k], recv_sem=rsem.at[k],
            device_id=to, device_id_type=MESH,
        )
        d.start()
        sent[key] = d
        leaving.append(d)

    def got(*keys):
        while len(leaving) > 40:
            leaving.pop(0).wait_send()
        for key in keys:
            if key not in waited:
                waited.add(key)
                sent[key].wait_recv()

    loads = [
        pltpu.make_async_copy(tok_in, io_buf.at[0], lsem.at[0]),
        pltpu.make_async_copy(cot_in, io_buf.at[1], lsem.at[1]),
        pltpu.make_async_copy(gw_in, wcat.at[:, pl.ds(0, FH)], lsem.at[2]),
        pltpu.make_async_copy(uw_in, wcat.at[:, pl.ds(FH, FH)], lsem.at[3]),
        pltpu.make_async_copy(dw_in, wd, lsem.at[4]),
    ]
    for d in loads:
        d.start()
    stores = []

    barrier = pltpu.get_barrier_semaphore()
    peers = [RIGHT, LEFT, YH, SIB, YL, ZL(1, 1), ZL(7, 1)] + [ZL(dz) for dz in range(1, 8)]
    for to in peers:
        pl.semaphore_signal(barrier, inc=1, device_id=to, device_id_type=MESH)

    def pack(v):
        v = v.astype(F32)
        return jnp.concatenate([v[:, :512], v[:, 512:]], axis=0).astype(BF)

    def unpack(v):
        v = v.astype(F32)
        return jnp.concatenate([v[:OWN], v[OWN:]], axis=1)

    for a in range(2):
        loads[a].wait()
        slot_o[a, SELF, 0] = pack(io_buf[a])
    pl.semaphore_wait(barrier, len(peers))

    def at(dz):
        return DZ.index(dz % 8)

    def hop_r(a, d, dl):
        send(("r", a, d, dl), slot_o.at[a, at(1 - d), dl], slot_o.at[a, at(-d), dl], ZL(1))

    def hop_l(a, d, dl):
        send(("l", a, d, dl), slot_o.at[a, at(d - 1), dl], slot_o.at[a, at(d), dl], ZL(7))

    def t_ag(a):
        send(("yl", a), slot_o.at[a, SELF, 0], slot_o.at[a, SELF, 1], YL)
        for dl, right, left in ((0, ZL(1), ZL(7)), (1, ZL(1, 1), ZL(7, 1))):
            send(("r", a, 1, dl), slot_o.at[a, SELF, 0], slot_o.at[a, at(7), dl], right)
            send(("l", a, 1, dl), slot_o.at[a, SELF, 0], slot_o.at[a, at(1), dl], left)

    def t_agy(a):
        got(("yl", a))
        send(("sh", a, SELF), slot_o.at[a, SELF], slot_s.at[a, SELF], SIB)

    def t_agz(a, d):
        for dl in range(2):
            if d < 4 or dl == 0:
                got(("r", a, d, dl))
            if d < 3 or (d == 3 and dl == 0):
                hop_r(a, d + 1, dl)
            if d < 4 or dl == 1:
                got(("l", a, d, dl))
            if d < 3 or (d == 3 and dl == 1):
                hop_l(a, d + 1, dl)
        for q in (at(-d), at(d))[: 2 if d < 4 else 1]:
            send(("sh", a, q), slot_o.at[a, q], slot_s.at[a, q], SIB)

    def t_asm(a, q):
        got(("sh", a, q))
        ref = (tok, cot)[a]
        for dl in range(2):
            v = jnp.concatenate([unpack(slot_o[a, q, dl]), unpack(slot_s[a, q, dl])], axis=0)
            ref[pl.ds(q * 96 + dl * CH, CH), :] = v.astype(BF)

    def masked(ref, mask, rows, cols, col0):
        def body(i):
            r = pl.ds(i * 128, 128)
            for k in range(cols):
                cs = pl.ds(col0 + k * 128, 128)
                ref[r, cs] = (ref[r, cs].astype(F32) * mask[i, k].astype(F32)).astype(BF)
        loop(rows, body)

    def t_mgu():
        loads[2].wait()
        masked(wcat, gm, 8, 7, 0)
        loads[3].wait()
        masked(wcat, um, 8, 7, FH)

    def t_md():
        loads[4].wait()
        masked(wd, dm, 7, 8, 0)

    def rows_x(j, xi):
        return pl.ds(pl.multiple_of(OFF[j] + xi * (CS[j] // 4), CS[j] // 4), CS[j] // 4)

    def rows_p(j, xi, hi):
        return pl.ds(pl.multiple_of(OFF[j] + xi * (CS[j] // 4) + hi * (CS[j] // 8), CS[j] // 8), CS[j] // 8)

    G, U = pl.ds(0, FH), pl.ds(FH, FH)
    A, B = pl.ds(0, CA), pl.ds(CA, FH - CA)

    def t_gu(j):
        rows = pl.ds(OFF[j], CS[j])

        def body(n):
            cs = pl.ds(n * 256, 256)
            p_gu[rows, cs] = dot_nn(tok[rows, :], wcat[:, cs]).astype(BF)
        loop(7, body)
        send(("g1", j), p_gu.at[rows_x(j, xf), G], b["f1g", j], RIGHT)
        send(("u1", j), p_gu.at[rows_x(j, xf), U], b["f1u", j], LEFT)
        send(("g2l", j), p_gu.at[rows_x(j, xl), G], b["f2g", j].at[1], LEFT)
        send(("u2r", j), p_gu.at[rows_x(j, xr), U], b["f2u", j].at[0], RIGHT)

    def t_hd(j):
        rows, p_h, pr = pl.ds(OFF[j], CS[j]), b["p_h", j], CS[j] // 8

        def body(n):
            cs = pl.ds(n * 256, 256)
            p_h[:, :, :, cs] = dot_nt(cot[rows, :], wd[cs, :]).astype(BF).reshape(4, 2, pr, 256)
        loop(3, body)
        cs = pl.ds(768, 128)
        p_h[:, :, :, cs] = dot_nt(cot[rows, :], wd[cs, :]).astype(BF).reshape(4, 2, pr, 128)
        send(("hy", j), p_h.at[:, oh], b["fy_h", j], YH)

    def add_to(ref, at_, other):
        ref[at_] = (ref[at_].astype(F32) + other[...].astype(F32)).astype(BF)

    def t_gu1(j):
        got(("g1", j))
        rows = rows_x(j, xr)
        add_to(p_gu, (rows, G), b["f1g", j])
        send(("g2r", j), p_gu.at[rows, G], b["f2g", j].at[0], RIGHT)
        got(("u1", j))
        rows = rows_x(j, xl)
        add_to(p_gu, (rows, U), b["f1u", j])
        send(("u2l", j), p_gu.at[rows, U], b["f2u", j].at[1], LEFT)

    def t_hd1(j):
        p_h, f2h = b["p_h", j], b["f2h", j]
        got(("hy", j))
        for xi in range(4):
            add_to(p_h, (xi, h), b["fy_h", j].at[xi])
        send(("h1a", j), p_h.at[xf, h, :, A], b["f1a", j], RIGHT)
        send(("h1b", j), p_h.at[xf, h, :, B], b["f1b", j], LEFT)
        send(("h2rb", j), p_h.at[xr, h, :, B], f2h.at[0, :, B], RIGHT)
        send(("h2la", j), p_h.at[xl, h, :, A], f2h.at[1, :, A], LEFT)

    def t_hd2(j):
        p_h, f2h = b["p_h", j], b["f2h", j]
        got(("h1a", j))
        add_to(p_h, (xr, h, slice(None), A), b["f1a", j])
        send(("h2ra", j), p_h.at[xr, h, :, A], f2h.at[0, :, A], RIGHT)
        got(("h1b", j))
        add_to(p_h, (xl, h, slice(None), B), b["f1b", j])
        send(("h2lb", j), p_h.at[xl, h, :, B], f2h.at[1, :, B], LEFT)

    def t_gu2(j):
        pr = CS[j] // 8
        got(("g2l", j), ("u2r", j), ("g2r", j), ("u2l", j))
        for f2, cs in ((b["f2g", j], G), (b["f2u", j], U)):
            def total(hi):
                r = pl.ds(pl.multiple_of(hi * pr, pr), pr)
                return p_gu[rows_p(j, x, hi), cs].astype(F32) + f2[0, r, :].astype(F32) + f2[1, r, :].astype(F32)
            b["sy_gu", j][:, cs] = total(oh).astype(BF)
            b["own_gu", j][:, cs] = total(h)
        send(("guy", j), b["sy_gu", j], b["fy_gu", j], YH)

    def steps(j, body):
        def at_(i):
            r = pl.ds(i * 16, 16)
            rr = pl.ds(pl.multiple_of(OFF[j] + x * (CS[j] // 4) + h * (CS[j] // 8) + i * 16, 16), 16)
            body(r, rr)
        loop(CS[j] // 128, at_)

    def t_act(j):
        got(("guy", j))
        own_gu, fy_gu = b["own_gu", j], b["fy_gu", j]

        def body(r, rr):
            pre_gate = own_gu[r, G] + fy_gu[r, G].astype(F32)
            pre_up = own_gu[r, U] + fy_gu[r, U].astype(F32)
            own_gu[r, G] = pre_gate
            own_gu[r, U] = pre_up
            hid[rr, :] = (pre_gate * jax.nn.sigmoid(pre_gate) * pre_up).astype(BF)
        steps(j, body)
        mine = rows_p(j, x, h)
        send(("hr", j), hid.at[mine], hid.at[mine], RIGHT)
        send(("hl", j), hid.at[mine], hid.at[mine], LEFT)
        send(("hy0", j), hid.at[mine], hid.at[mine], YH)

    def t_act2(j):
        got(("h2rb", j), ("h2la", j), ("h2ra", j), ("h2lb", j))
        own_gu, p_h, f2h = b["own_gu", j], b["p_h", j], b["f2h", j]

        def body(r, rr):
            pre_gate, pre_up = own_gu[r, G], own_gu[r, U]
            grad_hidden = p_h[x, h, r, :].astype(F32) + f2h[0, r, :].astype(F32) + f2h[1, r, :].astype(F32)
            sig = jax.nn.sigmoid(pre_gate)
            gp[rr, G] = (grad_hidden * pre_up * sig * (1.0 + pre_gate * (1.0 - sig))).astype(BF)
            gp[rr, U] = (grad_hidden * (pre_gate * sig)).astype(BF)
        steps(j, body)
        mine = rows_p(j, x, h)
        send(("py", j), gp.at[mine], gp.at[mine], YH)
        send(("pr0", j), gp.at[mine], gp.at[mine], RIGHT)
        send(("pl0", j), gp.at[mine], gp.at[mine], LEFT)

    def t_hx(j):
        fl, fr = rows_p(j, xl, h), rows_p(j, xr, h)
        got(("hr", j))
        send(("hfr", j), hid.at[fl, A], hid.at[fl, A], RIGHT)
        got(("hl", j))
        send(("hfl", j), hid.at[fr, B], hid.at[fr, B], LEFT)
        send(("hyl", j), hid.at[fl], hid.at[fl], YH)
        send(("hyr", j), hid.at[fr], hid.at[fr], YH)

    def t_hf(j):
        got(("hfr", j), ("hfl", j))
        ff = rows_p(j, xf, h)
        send(("hyf", j), hid.at[ff], hid.at[ff], YH)

    def t_py(j):
        got(("py", j))
        other = rows_p(j, x, oh)
        send(("pr1", j), gp.at[other], gp.at[other], RIGHT)
        send(("pl1", j), gp.at[other], gp.at[other], LEFT)

    def t_pf(j, k):
        fl, fr = rows_p(j, xl, (h, oh)[k]), rows_p(j, xr, (h, oh)[k])
        got((("pr0", "pr1")[k], j))
        send(("pfr", j, k), gp.at[fl, G], gp.at[fl, G], RIGHT)
        got((("pl0", "pl1")[k], j))
        send(("pfl", j, k), gp.at[fr, U], gp.at[fr, U], LEFT)

    def t_d(a, j):
        if a == 0:
            got(("hy0", j), ("hyl", j), ("hyr", j), ("hyf", j))
        else:
            got(("pfr", j, 0), ("pfl", j, 0), ("pfr", j, 1), ("pfl", j, 1))
        p0, p1 = DONE[j], DONE[j + 1]
        n_p = p1 - p0
        rows = pl.ds(p0 * 96, n_p * 96)

        def body(n):
            cs = pl.ds(n * 256, 256)
            er = pl.ds((n // 2) * OWN, OWN)
            ec = pl.ds((n % 2) * 256, 256)
            v = dot_nn(hid[rows, :], wd[:, cs]) if a == 0 else dot_nt(gp[rows, :], wcat[cs, :])
            v = v.reshape(n_p, 2, 2, OWN, 256)
            for p in range(n_p):
                for dl in range(2):
                    e_own[a, dl, p0 + p, er, ec] = v[p, dl, 0]
                    e_sib[a, dl, p0 + p, er, ec] = v[p, dl, 1]
        loop(4, body)
        for dl in (1, 0):
            for p in range(p0, p1):
                e_sb[a, dl, p] = e_sib[a, dl, p].astype(BF)
            ps = pl.ds(p0, n_p)
            send(("es", a, j, dl), e_sb.at[a, dl, ps], e_sr.at[a, dl, ps], SIB)

    def to_z(a, p, dl, v):
        if p == SELF:
            e_own[a, dl, p] = v
        else:
            b["ez_s"][a, p, dl] = v.astype(BF)
            send(("ez", a, p, dl), b["ez_s"].at[a, p, dl], b["ez_r"].at[a, p, dl], ZL(DZ[p]))

    def t_ea(a, j):
        p0, p1 = DONE[j], DONE[j + 1]
        if YFIRST[j]:
            got(("es", a, j, 1))
            for p in range(p0, p1):
                b["ey_s"][a, p] = (e_own[a, 1, p] + e_sr[a, 1, p].astype(F32)).astype(BF)
            ps = pl.ds(p0, p1 - p0)
            send(("ey", a, j), b["ey_s"].at[a, ps], b["ey_r"].at[a, ps], YL)
        else:
            for dl in (1, 0):
                got(("es", a, j, dl))
                for p in range(p0, p1):
                    to_z(a, p, dl, e_own[a, dl, p] + e_sr[a, dl, p].astype(F32))

    def t_eb(a, j):
        got(("es", a, j, 0), ("ey", a, j))
        for p in range(DONE[j], DONE[j + 1]):
            to_z(a, p, 0, e_own[a, 0, p] + e_sr[a, 0, p].astype(F32) + b["ey_r"][a, p].astype(F32))

    ZF = [p for j in range(NCH) for p in range(DONE[j], DONE[j + 1]) if not YFIRST[j]]

    def whole(a, dl, pairs):
        v = e_own[a, dl, SELF] if SELF in pairs else None
        for p in pairs:
            if p != SELF:
                got(("ez", a, p, dl))
                t = b["ez_r"][a, p, dl].astype(F32)
                v = t if v is None else v + t
        return v

    def t_f1(a):
        b["ef_s"][a] = whole(a, 1, ZF).astype(BF)
        send(("ef", a), b["ef_s"].at[a], b["ef_r"].at[a], YL)

    def t_f2(a):
        v = whole(a, 0, range(8))
        if ZF:
            got(("ef", a))
            v = v + b["ef_r"][a].astype(F32)
        (mix_out, gt_out)[a][...] = jnp.concatenate([v[:OWN], v[OWN:]], axis=1).astype(BF)

    scale = 1.0 / math.sqrt(TOK)

    def store(k, src, dst, rows):
        d = pltpu.make_async_copy(src.at[rows], dst.at[rows], lsem.at[k])
        d.start()
        stores.append(d)

    def t_wgp(n):
        for i in (2 * n, 2 * n + 1):
            cs = pl.ds(i * 128, 128)
            v = dot_tn(tok[:, cs], gp[...]) * scale
            for k in range(7):
                ks = pl.ds(k * 128, 128)
                b["gg_b"][cs, ks] = (v[:, k * 128:(k + 1) * 128] * gm[i, k].astype(F32)).astype(BF)
                b["gu_b"][cs, ks] = (v[:, FH + k * 128:FH + (k + 1) * 128] * um[i, k].astype(F32)).astype(BF)
        store(3 * n, b["gg_b"], gg_out, pl.ds(n * 256, 256))
        store(3 * n + 1, b["gu_b"], gu_out, pl.ds(n * 256, 256))

    def t_wd(n):
        blocks = range(2 * n, min(2 * n + 2, 7))
        for i in blocks:
            cs = pl.ds(i * 128, 128)
            v = dot_tn(hid[:, cs], cot[...]) * scale
            for k in range(8):
                ks = pl.ds(k * 128, 128)
                b["gd_b"][cs, ks] = (v[:, k * 128:(k + 1) * 128] * dm[i, k].astype(F32)).astype(BF)
        store(3 * n + 2, b["gd_b"], gd_out, pl.ds(n * 256, len(blocks) * 128))

    do = dict(
        ag=t_ag, agy=t_agy, agz=t_agz, asm=t_asm, mgu=t_mgu, md=t_md, gu=t_gu, hd=t_hd, gu1=t_gu1, hd1=t_hd1, hd2=t_hd2,
        gu2=t_gu2, act=t_act, act2=t_act2, hx=t_hx, hf=t_hf, py=t_py, pf=t_pf, d=t_d, ea=t_ea, eb=t_eb, f1=t_f1, f2=t_f2,
        wgp=t_wgp, wd=t_wd,
    )
    for name, *which in ORDER:
        do[name](*which)
    for d in leaving:
        d.wait_send()
    for d in stores:
        d.wait()


def hand_on(*refs):
    ins, outs, held, (in_sem, out_sem) = refs[:5], refs[5:10], refs[10:15], refs[15:]
    reads, writes = [], []
    for k in (2, 3, 4, 0, 1):
        n = 4 if ins[k].shape[0] > OWN else 1
        for i in range(n):
            r = pl.ds(i * (ins[k].shape[0] // n), ins[k].shape[0] // n)
            t = len(reads)
            reads.append(pltpu.make_async_copy(ins[k].at[r], held[k].at[r], in_sem.at[t]))
            writes.append(pltpu.make_async_copy(held[k].at[r], outs[k].at[r], out_sem.at[t]))
            reads[t].start()
    for read, write in zip(reads, writes):
        read.wait()
        write.start()
    for write in writes:
        write.wait()


def on_device(tokens, gate_weight, up_weight, down_weight, gate_mask, up_mask, down_mask, grad_out):
    vm = pl.BlockSpec(memory_space=pltpu.VMEM)
    sm = pl.BlockSpec(memory_space=pltpu.SMEM)
    hbm = pl.BlockSpec(memory_space=pl.ANY)
    n_msg = 46 + NCH * 37 + 2 * 14 + 2
    D, V = pltpu.SemaphoreType.DMA, pltpu.VMEM
    outs = pl.pallas_call(
        kernel,
        out_shape=(
            jax.ShapeDtypeStruct((OWN, W), BF),
            jax.ShapeDtypeStruct((OWN, W), BF),
            jax.ShapeDtypeStruct((W, FH), BF),
            jax.ShapeDtypeStruct((W, FH), BF),
            jax.ShapeDtypeStruct((FH, W), BF),
        ),
        in_specs=[hbm, hbm, hbm, hbm, sm, sm, sm, hbm],
        out_specs=(vm, vm, hbm, hbm, hbm),
        scratch_shapes=[*buffers().values(), D((12,)), D((n_msg,)), D((n_msg,))],
        name="layer",
        compiler_params=pltpu.CompilerParams(
            collective_id=0, has_side_effects=True, vmem_limit_bytes=60 << 20
        ),
        cost_estimate=pl.CostEstimate(flops=9 * 2 * TOK * W * FH, bytes_accessed=12 << 20, transcendentals=TOK * FH),
    )(tokens, gate_weight, up_weight, down_weight, gate_mask, up_mask, down_mask, grad_out)
    return pl.pallas_call(
        hand_on,
        out_shape=tuple(jax.ShapeDtypeStruct(o.shape, o.dtype) for o in outs),
        in_specs=[hbm] * 5,
        out_specs=(hbm,) * 5,
        scratch_shapes=[V(o.shape, o.dtype) for o in outs] + [D((14,)), D((14,))],
        name="hand_on",
        compiler_params=pltpu.CompilerParams(vmem_limit_bytes=60 << 20),
        cost_estimate=pl.CostEstimate(flops=0, bytes_accessed=12 << 20, transcendentals=0),
    )(*outs)


def solution(mesh):
    placed = (
        P("mp", "seq"),
        P("seq", "mp"),
        P("seq", "mp"),
        P("mp", "seq"),
        P("seq", "mp"),
        P("seq", "mp"),
        P("mp", "seq"),
        P("mp", "seq"),
    )
    return jax.shard_map(
        on_device,
        mesh=mesh,
        in_specs=placed,
        out_specs=(P("mp", "seq"), P("mp", "seq"), P("seq", "mp"), P("seq", "mp"), P("mp", "seq")),
        check_vma=False,
    )
```

```python
import math

import jax
import jax.numpy as jnp
from jax import lax
from jax.experimental import pallas as pl
from jax.experimental.pallas import tpu as pltpu
from jax.sharding import PartitionSpec as P

MESH = pl.DeviceIdType.MESH
BF = jnp.bfloat16
F32 = jnp.float32

TOK = 768
W = 1024
FH = 896
OWN = 24
CH = 48
CA = 512
CS = (128, 256, 256, 128)
DZ = (1, 0, 7, 2, 4, 5, 3, 6)
YFIRST = (False, False, True, True)
ORDER = (
    ("ag", 0), ("md",), ("ag", 1), ("mgu",), ("agy", 0), ("agy", 1), ("agz", 0, 1), ("asm", 0, 1), ("agz", 1, 1),
    ("asm", 0, 0), ("gu", 0), ("asm", 1, 2), ("agz", 0, 2), ("asm", 1, 0), ("asm", 0, 2), ("asm", 1, 1), ("hd", 0),
    ("agz", 1, 2), ("gu1", 0), ("asm", 0, 3), ("gu", 1), ("asm", 1, 3), ("agz", 0, 3), ("hd", 1), ("agz", 1, 3),
    ("asm", 0, 6), ("hd1", 0), ("gu2", 0), ("asm", 1, 7), ("agz", 0, 4), ("gu1", 1), ("asm", 1, 6), ("asm", 0, 5),
    ("agz", 1, 4), ("asm", 0, 4), ("gu", 2), ("asm", 1, 5), ("asm", 1, 4), ("hd", 2), ("hd2", 0), ("hd1", 1),
    ("gu2", 1), ("gu1", 2), ("hd", 3), ("act", 0), ("act2", 0), ("asm", 0, 7), ("gu", 3), ("gu2", 2), ("hx", 0),
    ("act", 1), ("hd2", 1), ("hd1", 2), ("gu1", 3), ("hf", 0), ("hx", 1), ("hd1", 3), ("hd2", 2), ("act2", 1),
    ("hf", 1), ("act", 2), ("py", 0), ("gu2", 3), ("d", 0, 0), ("act2", 2), ("hx", 2), ("py", 1), ("pf", 0, 1),
    ("d", 0, 1), ("hd2", 3), ("ea", 0, 0), ("hf", 2), ("pf", 0, 0), ("act", 3), ("pf", 1, 0), ("pf", 1, 1),
    ("ea", 0, 1), ("py", 2), ("d", 1, 0), ("hx", 3), ("act2", 3), ("pf", 2, 0), ("d", 0, 2), ("d", 1, 1),
    ("pf", 2, 1), ("ea", 1, 0), ("ea", 0, 2), ("pf", 3, 0), ("py", 3), ("hf", 3), ("ea", 1, 1), ("d", 1, 2),
    ("pf", 3, 1), ("eb", 0, 2), ("ea", 1, 2), ("d", 0, 3), ("d", 1, 3), ("ea", 0, 3), ("eb", 1, 2), ("wgp", 3),
    ("ea", 1, 3), ("eb", 0, 3), ("wd", 0), ("eb", 1, 3), ("f1", 1), ("wd", 1), ("f1", 0), ("wgp", 2), ("wd", 3),
    ("wgp", 0), ("wd", 2), ("f2", 0), ("wgp", 1), ("f2", 1),
)

NCH = len(CS)
OFF = [sum(CS[:j]) for j in range(NCH + 1)]
NEG = tuple(DZ.index((8 - d) % 8) for d in DZ)
SELF = DZ.index(0)
DONE = [o // 96 for o in OFF]


def dot_nn(a, b):
    return jnp.dot(a, b, preferred_element_type=F32)


def dot_nt(a, b):
    return lax.dot_general(a, b, (((1,), (1,)), ((), ())), preferred_element_type=F32)


def dot_tn(a, b):
    return lax.dot_general(a, b, (((0,), (0,)), ((), ())), preferred_element_type=F32)


def loop(n, body):
    for i in range(n):
        body(i)


def buffers():
    V = pltpu.VMEM
    b = dict(
        wcat=V((W, 2 * FH), BF), wd=V((FH, W), BF), io_buf=V((2, OWN, W), BF),
        slot_o=V((2, 8, 2, CH, 512), BF), slot_s=V((2, 8, 2, CH, 512), BF),
        tok=V((TOK, W), BF), cot=V((TOK, W), BF),
        p_gu=V((TOK, 2 * FH), BF), hid=V((TOK, FH), BF), gp=V((TOK, 2 * FH), BF),
        e_own=V((2, 2, 8, CH, 512), F32), e_sib=V((2, 2, 8, CH, 512), F32),
        e_sb=V((2, 2, 8, CH, 512), BF), e_sr=V((2, 2, 8, CH, 512), BF),
        ey_s=V((2, 8, CH, 512), BF), ey_r=V((2, 8, CH, 512), BF),
        ez_s=V((2, 8, 2, CH, 512), BF), ez_r=V((2, 8, 2, CH, 512), BF),
        ef_s=V((2, CH, 512), BF), ef_r=V((2, CH, 512), BF),
        gg_b=V((W, FH), BF), gu_b=V((W, FH), BF), gd_b=V((FH, W), BF),
    )
    for j, r in enumerate(CS):
        pr, xr = r // 8, r // 4
        b.update({
            ("p_h", j): V((4, 2, pr, FH), BF), ("fy_h", j): V((4, pr, FH), BF),
            ("f1g", j): V((xr, FH), BF), ("f1u", j): V((xr, FH), BF),
            ("f2g", j): V((2, xr, FH), BF), ("f2u", j): V((2, xr, FH), BF),
            ("own_gu", j): V((pr, 2 * FH), F32), ("sy_gu", j): V((pr, 2 * FH), BF),
            ("fy_gu", j): V((pr, 2 * FH), BF),
            ("f1a", j): V((pr, CA), BF), ("f1b", j): V((pr, FH - CA), BF),
            ("f2h", j): V((2, pr, FH), BF),
        })
    return b


def kernel(*refs):
    (tok_in, gw_in, uw_in, dw_in, gm, um, dm, cot_in, mix_out, gt_out, gg_out, gu_out, gd_out) = refs[:13]
    b = dict(zip(buffers(), refs[13:-3]))
    lsem, ssem, rsem = refs[-3:]
    wcat, wd, io_buf, slot_o, slot_s = (b[k] for k in ("wcat", "wd", "io_buf", "slot_o", "slot_s"))
    tok, cot, p_gu, hid, gp = (b[k] for k in ("tok", "cot", "p_gu", "hid", "gp"))
    e_own, e_sib, e_sb, e_sr = (b[k] for k in ("e_own", "e_sib", "e_sb", "e_sr"))

    s = lax.axis_index("seq")
    m = lax.axis_index("mp")
    h, x = s // 4, s % 4
    l, z, c = m // 16, (m // 2) % 8, m % 2
    xr, xl, xf = (x + 1) % 4, (x + 3) % 4, (x + 2) % 4
    oh = 1 - h

    def mp_of(dz, dl, dc=0):
        return ((l + dl) % 2) * 16 + ((z + dz) % 8) * 2 + (c + dc) % 2

    RIGHT, LEFT, YH = (h * 4 + xr, m), (h * 4 + xl, m), (oh * 4 + x, m)
    SIB, YL = (s, mp_of(0, 0, 1)), (s, mp_of(0, 1))

    def ZL(dz, dl=0):
        return (s, mp_of(dz, dl))

    sent, waited, leaving = {}, set(), []

    def send(key, src, dst, to):
        k = len(sent)
        d = pltpu.make_async_remote_copy(
            src_ref=src, dst_ref=dst, send_sem=ssem.at[k], recv_sem=rsem.at[k],
            device_id=to, device_id_type=MESH,
        )
        d.start()
        sent[key] = d
        leaving.append(d)

    def got(*keys):
        while len(leaving) > 20:
            leaving.pop(0).wait_send()
        for key in keys:
            if key not in waited:
                waited.add(key)
                sent[key].wait_recv()

    barrier = pltpu.get_barrier_semaphore()
    peers = [RIGHT, LEFT, YH, SIB, YL, ZL(1, 1), ZL(7, 1)] + [ZL(dz) for dz in range(1, 8)]
    for to in peers:
        pl.semaphore_signal(barrier, inc=1, device_id=to, device_id_type=MESH)

    loads = [
        pltpu.make_async_copy(tok_in, io_buf.at[0], lsem.at[0]),
        pltpu.make_async_copy(cot_in, io_buf.at[1], lsem.at[1]),
        pltpu.make_async_copy(gw_in, wcat.at[:, pl.ds(0, FH)], lsem.at[2]),
        pltpu.make_async_copy(uw_in, wcat.at[:, pl.ds(FH, FH)], lsem.at[3]),
        pltpu.make_async_copy(dw_in, wd, lsem.at[4]),
    ]
    for d in loads:
        d.start()
    stores = []

    def pack(v):
        v = v.astype(F32)
        return jnp.concatenate([v[:, :512], v[:, 512:]], axis=0).astype(BF)

    def unpack(v):
        v = v.astype(F32)
        return jnp.concatenate([v[:OWN], v[OWN:]], axis=1)

    for a in range(2):
        loads[a].wait()
        slot_o[a, SELF, 0] = pack(io_buf[a])
    pl.semaphore_wait(barrier, len(peers))

    def at(dz):
        return DZ.index(dz % 8)

    def hop_r(a, d, dl):
        send(("r", a, d, dl), slot_o.at[a, at(1 - d), dl], slot_o.at[a, at(-d), dl], ZL(1))

    def hop_l(a, d, dl):
        send(("l", a, d, dl), slot_o.at[a, at(d - 1), dl], slot_o.at[a, at(d), dl], ZL(7))

    def t_ag(a):
        send(("yl", a), slot_o.at[a, SELF, 0], slot_o.at[a, SELF, 1], YL)
        for dl, right, left in ((0, ZL(1), ZL(7)), (1, ZL(1, 1), ZL(7, 1))):
            send(("r", a, 1, dl), slot_o.at[a, SELF, 0], slot_o.at[a, at(7), dl], right)
            send(("l", a, 1, dl), slot_o.at[a, SELF, 0], slot_o.at[a, at(1), dl], left)

    def t_agy(a):
        got(("yl", a))
        send(("sh", a, SELF), slot_o.at[a, SELF], slot_s.at[a, SELF], SIB)

    def t_agz(a, d):
        for dl in range(2):
            if d < 4 or dl == 0:
                got(("r", a, d, dl))
            if d < 3 or (d == 3 and dl == 0):
                hop_r(a, d + 1, dl)
            if d < 4 or dl == 1:
                got(("l", a, d, dl))
            if d < 3 or (d == 3 and dl == 1):
                hop_l(a, d + 1, dl)
        for q in (at(-d), at(d))[: 2 if d < 4 else 1]:
            send(("sh", a, q), slot_o.at[a, q], slot_s.at[a, q], SIB)

    def t_asm(a, q):
        got(("sh", a, q))
        ref = (tok, cot)[a]
        for dl in range(2):
            v = jnp.concatenate([unpack(slot_o[a, q, dl]), unpack(slot_s[a, q, dl])], axis=0)
            ref[pl.ds(q * 96 + dl * CH, CH), :] = v.astype(BF)

    def masked(ref, mask, rows, cols, col0):
        def body(i):
            r = pl.ds(i * 128, 128)
            for k in range(cols):
                cs = pl.ds(col0 + k * 128, 128)
                ref[r, cs] = (ref[r, cs].astype(F32) * mask[i, k].astype(F32)).astype(BF)
        loop(rows, body)

    def t_mgu():
        loads[2].wait()
        masked(wcat, gm, 8, 7, 0)
        loads[3].wait()
        masked(wcat, um, 8, 7, FH)

    def t_md():
        loads[4].wait()
        masked(wd, dm, 7, 8, 0)

    def rows_x(j, xi):
        return pl.ds(pl.multiple_of(OFF[j] + xi * (CS[j] // 4), CS[j] // 4), CS[j] // 4)

    def rows_p(j, xi, hi):
        return pl.ds(pl.multiple_of(OFF[j] + xi * (CS[j] // 4) + hi * (CS[j] // 8), CS[j] // 8), CS[j] // 8)

    G, U = pl.ds(0, FH), pl.ds(FH, FH)
    A, B = pl.ds(0, CA), pl.ds(CA, FH - CA)

    def t_gu(j):
        rows = pl.ds(OFF[j], CS[j])

        def body(n):
            cs = pl.ds(n * 256, 256)
            p_gu[rows, cs] = dot_nn(tok[rows, :], wcat[:, cs]).astype(BF)
        loop(7, body)
        send(("g1", j), p_gu.at[rows_x(j, xf), G], b["f1g", j], RIGHT)
        send(("u1", j), p_gu.at[rows_x(j, xf), U], b["f1u", j], LEFT)
        send(("g2l", j), p_gu.at[rows_x(j, xl), G], b["f2g", j].at[1], LEFT)
        send(("u2r", j), p_gu.at[rows_x(j, xr), U], b["f2u", j].at[0], RIGHT)

    def t_hd(j):
        rows, p_h, pr = pl.ds(OFF[j], CS[j]), b["p_h", j], CS[j] // 8

        def body(n):
            cs = pl.ds(n * 256, 256)
            p_h[:, :, :, cs] = dot_nt(cot[rows, :], wd[cs, :]).astype(BF).reshape(4, 2, pr, 256)
        loop(3, body)
        cs = pl.ds(768, 128)
        p_h[:, :, :, cs] = dot_nt(cot[rows, :], wd[cs, :]).astype(BF).reshape(4, 2, pr, 128)
        send(("hy", j), p_h.at[:, oh], b["fy_h", j], YH)

    def add_to(ref, at_, other):
        ref[at_] = (ref[at_].astype(F32) + other[...].astype(F32)).astype(BF)

    def t_gu1(j):
        got(("g1", j))
        rows = rows_x(j, xr)
        add_to(p_gu, (rows, G), b["f1g", j])
        send(("g2r", j), p_gu.at[rows, G], b["f2g", j].at[0], RIGHT)
        got(("u1", j))
        rows = rows_x(j, xl)
        add_to(p_gu, (rows, U), b["f1u", j])
        send(("u2l", j), p_gu.at[rows, U], b["f2u", j].at[1], LEFT)

    def t_hd1(j):
        p_h, f2h = b["p_h", j], b["f2h", j]
        got(("hy", j))
        for xi in range(4):
            add_to(p_h, (xi, h), b["fy_h", j].at[xi])
        send(("h1a", j), p_h.at[xf, h, :, A], b["f1a", j], RIGHT)
        send(("h1b", j), p_h.at[xf, h, :, B], b["f1b", j], LEFT)
        send(("h2rb", j), p_h.at[xr, h, :, B], f2h.at[0, :, B], RIGHT)
        send(("h2la", j), p_h.at[xl, h, :, A], f2h.at[1, :, A], LEFT)

    def t_hd2(j):
        p_h, f2h = b["p_h", j], b["f2h", j]
        got(("h1a", j))
        add_to(p_h, (xr, h, slice(None), A), b["f1a", j])
        send(("h2ra", j), p_h.at[xr, h, :, A], f2h.at[0, :, A], RIGHT)
        got(("h1b", j))
        add_to(p_h, (xl, h, slice(None), B), b["f1b", j])
        send(("h2lb", j), p_h.at[xl, h, :, B], f2h.at[1, :, B], LEFT)

    def t_gu2(j):
        pr = CS[j] // 8
        got(("g2l", j), ("u2r", j), ("g2r", j), ("u2l", j))
        for f2, cs in ((b["f2g", j], G), (b["f2u", j], U)):
            def total(hi):
                r = pl.ds(pl.multiple_of(hi * pr, pr), pr)
                return p_gu[rows_p(j, x, hi), cs].astype(F32) + f2[0, r, :].astype(F32) + f2[1, r, :].astype(F32)
            b["sy_gu", j][:, cs] = total(oh).astype(BF)
            b["own_gu", j][:, cs] = total(h)
        send(("guy", j), b["sy_gu", j], b["fy_gu", j], YH)

    def steps(j, body):
        def at_(i):
            r = pl.ds(i * 16, 16)
            rr = pl.ds(pl.multiple_of(OFF[j] + x * (CS[j] // 4) + h * (CS[j] // 8) + i * 16, 16), 16)
            body(r, rr)
        loop(CS[j] // 128, at_)

    def t_act(j):
        got(("guy", j))
        own_gu, fy_gu = b["own_gu", j], b["fy_gu", j]

        def body(r, rr):
            pre_gate = own_gu[r, G] + fy_gu[r, G].astype(F32)
            pre_up = own_gu[r, U] + fy_gu[r, U].astype(F32)
            own_gu[r, G] = pre_gate
            own_gu[r, U] = pre_up
            hid[rr, :] = (pre_gate * jax.nn.sigmoid(pre_gate) * pre_up).astype(BF)
        steps(j, body)
        mine = rows_p(j, x, h)
        send(("hr", j), hid.at[mine], hid.at[mine], RIGHT)
        send(("hl", j), hid.at[mine], hid.at[mine], LEFT)
        send(("hy0", j), hid.at[mine], hid.at[mine], YH)

    def t_act2(j):
        got(("h2rb", j), ("h2la", j), ("h2ra", j), ("h2lb", j))
        own_gu, p_h, f2h = b["own_gu", j], b["p_h", j], b["f2h", j]

        def body(r, rr):
            pre_gate, pre_up = own_gu[r, G], own_gu[r, U]
            grad_hidden = p_h[x, h, r, :].astype(F32) + f2h[0, r, :].astype(F32) + f2h[1, r, :].astype(F32)
            sig = jax.nn.sigmoid(pre_gate)
            gp[rr, G] = (grad_hidden * pre_up * sig * (1.0 + pre_gate * (1.0 - sig))).astype(BF)
            gp[rr, U] = (grad_hidden * (pre_gate * sig)).astype(BF)
        steps(j, body)
        mine = rows_p(j, x, h)
        send(("py", j), gp.at[mine], gp.at[mine], YH)
        send(("pr0", j), gp.at[mine], gp.at[mine], RIGHT)
        send(("pl0", j), gp.at[mine], gp.at[mine], LEFT)

    def t_hx(j):
        fl, fr = rows_p(j, xl, h), rows_p(j, xr, h)
        got(("hr", j))
        send(("hfr", j), hid.at[fl, A], hid.at[fl, A], RIGHT)
        got(("hl", j))
        send(("hfl", j), hid.at[fr, B], hid.at[fr, B], LEFT)
        send(("hyl", j), hid.at[fl], hid.at[fl], YH)
        send(("hyr", j), hid.at[fr], hid.at[fr], YH)

    def t_hf(j):
        got(("hfr", j), ("hfl", j))
        ff = rows_p(j, xf, h)
        send(("hyf", j), hid.at[ff], hid.at[ff], YH)

    def t_py(j):
        got(("py", j))
        other = rows_p(j, x, oh)
        send(("pr1", j), gp.at[other], gp.at[other], RIGHT)
        send(("pl1", j), gp.at[other], gp.at[other], LEFT)

    def t_pf(j, k):
        fl, fr = rows_p(j, xl, (h, oh)[k]), rows_p(j, xr, (h, oh)[k])
        got((("pr0", "pr1")[k], j))
        send(("pfr", j, k), gp.at[fl, G], gp.at[fl, G], RIGHT)
        got((("pl0", "pl1")[k], j))
        send(("pfl", j, k), gp.at[fr, U], gp.at[fr, U], LEFT)

    def t_d(a, j):
        if a == 0:
            got(("hy0", j), ("hyl", j), ("hyr", j), ("hyf", j))
        else:
            got(("pfr", j, 0), ("pfl", j, 0), ("pfr", j, 1), ("pfl", j, 1))
        p0, p1 = DONE[j], DONE[j + 1]
        n_p = p1 - p0
        rows = pl.ds(p0 * 96, n_p * 96)

        def body(n):
            cs = pl.ds(n * 256, 256)
            er = pl.ds((n // 2) * OWN, OWN)
            ec = pl.ds((n % 2) * 256, 256)
            v = dot_nn(hid[rows, :], wd[:, cs]) if a == 0 else dot_nt(gp[rows, :], wcat[cs, :])
            v = v.reshape(n_p, 2, 2, OWN, 256)
            for p in range(n_p):
                for dl in range(2):
                    e_own[a, dl, p0 + p, er, ec] = v[p, dl, 0]
                    e_sib[a, dl, p0 + p, er, ec] = v[p, dl, 1]
        loop(4, body)
        for dl in (1, 0):
            for p in range(p0, p1):
                e_sb[a, dl, p] = e_sib[a, dl, p].astype(BF)
            ps = pl.ds(p0, n_p)
            send(("es", a, j, dl), e_sb.at[a, dl, ps], e_sr.at[a, dl, ps], SIB)

    def to_z(a, p, dl, v):
        if p == SELF:
            e_own[a, dl, p] = v
        else:
            b["ez_s"][a, p, dl] = v.astype(BF)
            send(("ez", a, p, dl), b["ez_s"].at[a, p, dl], b["ez_r"].at[a, p, dl], ZL(DZ[p]))

    def t_ea(a, j):
        p0, p1 = DONE[j], DONE[j + 1]
        if YFIRST[j]:
            got(("es", a, j, 1))
            for p in range(p0, p1):
                b["ey_s"][a, p] = (e_own[a, 1, p] + e_sr[a, 1, p].astype(F32)).astype(BF)
            ps = pl.ds(p0, p1 - p0)
            send(("ey", a, j), b["ey_s"].at[a, ps], b["ey_r"].at[a, ps], YL)
        else:
            for dl in (1, 0):
                got(("es", a, j, dl))
                for p in range(p0, p1):
                    to_z(a, p, dl, e_own[a, dl, p] + e_sr[a, dl, p].astype(F32))

    def t_eb(a, j):
        got(("es", a, j, 0), ("ey", a, j))
        for p in range(DONE[j], DONE[j + 1]):
            to_z(a, p, 0, e_own[a, 0, p] + e_sr[a, 0, p].astype(F32) + b["ey_r"][a, p].astype(F32))

    ZF = [p for j in range(NCH) for p in range(DONE[j], DONE[j + 1]) if not YFIRST[j]]

    def whole(a, dl, pairs):
        v = e_own[a, dl, SELF] if SELF in pairs else None
        for p in pairs:
            if p != SELF:
                got(("ez", a, p, dl))
                t = b["ez_r"][a, p, dl].astype(F32)
                v = t if v is None else v + t
        return v

    def t_f1(a):
        b["ef_s"][a] = whole(a, 1, ZF).astype(BF)
        send(("ef", a), b["ef_s"].at[a], b["ef_r"].at[a], YL)

    def t_f2(a):
        v = whole(a, 0, range(8))
        if ZF:
            got(("ef", a))
            v = v + b["ef_r"][a].astype(F32)
        (mix_out, gt_out)[a][...] = jnp.concatenate([v[:OWN], v[OWN:]], axis=1).astype(BF)

    scale = 1.0 / math.sqrt(TOK)

    def store(k, src, dst, rows):
        d = pltpu.make_async_copy(src.at[rows], dst.at[rows], lsem.at[k])
        d.start()
        stores.append(d)

    def t_wgp(n):
        for i in (2 * n, 2 * n + 1):
            cs = pl.ds(i * 128, 128)
            v = dot_tn(tok[:, cs], gp[...]) * scale
            for k in range(7):
                ks = pl.ds(k * 128, 128)
                b["gg_b"][cs, ks] = (v[:, k * 128:(k + 1) * 128] * gm[i, k].astype(F32)).astype(BF)
                b["gu_b"][cs, ks] = (v[:, FH + k * 128:FH + (k + 1) * 128] * um[i, k].astype(F32)).astype(BF)
        store(3 * n, b["gg_b"], gg_out, pl.ds(n * 256, 256))
        store(3 * n + 1, b["gu_b"], gu_out, pl.ds(n * 256, 256))

    def t_wd(n):
        blocks = range(2 * n, min(2 * n + 2, 7))
        for i in blocks:
            cs = pl.ds(i * 128, 128)
            v = dot_tn(hid[:, cs], cot[...]) * scale
            for k in range(8):
                ks = pl.ds(k * 128, 128)
                b["gd_b"][cs, ks] = (v[:, k * 128:(k + 1) * 128] * dm[i, k].astype(F32)).astype(BF)
        store(3 * n + 2, b["gd_b"], gd_out, pl.ds(n * 256, len(blocks) * 128))

    do = dict(
        ag=t_ag, agy=t_agy, agz=t_agz, asm=t_asm, mgu=t_mgu, md=t_md, gu=t_gu, hd=t_hd, gu1=t_gu1, hd1=t_hd1, hd2=t_hd2,
        gu2=t_gu2, act=t_act, act2=t_act2, hx=t_hx, hf=t_hf, py=t_py, pf=t_pf, d=t_d, ea=t_ea, eb=t_eb, f1=t_f1, f2=t_f2,
        wgp=t_wgp, wd=t_wd,
    )
    for name, *which in ORDER:
        do[name](*which)
    for d in leaving:
        d.wait_send()
    for d in stores:
        d.wait()


def hand_on(*refs):
    ins, outs, held, (in_sem, out_sem) = refs[:5], refs[5:10], refs[10:15], refs[15:]
    reads, writes = [], []
    for k in (2, 3, 4, 0, 1):
        n = 4 if ins[k].shape[0] > OWN else 1
        for i in range(n):
            r = pl.ds(i * (ins[k].shape[0] // n), ins[k].shape[0] // n)
            t = len(reads)
            reads.append(pltpu.make_async_copy(ins[k].at[r], held[k].at[r], in_sem.at[t]))
            writes.append(pltpu.make_async_copy(held[k].at[r], outs[k].at[r], out_sem.at[t]))
            reads[t].start()
    for read, write in zip(reads, writes):
        read.wait()
        write.start()
    for write in writes:
        write.wait()


def on_device(tokens, gate_weight, up_weight, down_weight, gate_mask, up_mask, down_mask, grad_out):
    vm = pl.BlockSpec(memory_space=pltpu.VMEM)
    sm = pl.BlockSpec(memory_space=pltpu.SMEM)
    hbm = pl.BlockSpec(memory_space=pl.ANY)
    n_msg = 46 + NCH * 37 + 2 * 14 + 2
    D, V = pltpu.SemaphoreType.DMA, pltpu.VMEM
    outs = pl.pallas_call(
        kernel,
        out_shape=(
            jax.ShapeDtypeStruct((OWN, W), BF),
            jax.ShapeDtypeStruct((OWN, W), BF),
            jax.ShapeDtypeStruct((W, FH), BF),
            jax.ShapeDtypeStruct((W, FH), BF),
            jax.ShapeDtypeStruct((FH, W), BF),
        ),
        in_specs=[hbm, hbm, hbm, hbm, sm, sm, sm, hbm],
        out_specs=(vm, vm, hbm, hbm, hbm),
        scratch_shapes=[*buffers().values(), D((12,)), D((n_msg,)), D((n_msg,))],
        name="layer",
        compiler_params=pltpu.CompilerParams(
            collective_id=0, has_side_effects=True, vmem_limit_bytes=60 << 20
        ),
        cost_estimate=pl.CostEstimate(flops=9 * 2 * TOK * W * FH, bytes_accessed=12 << 20, transcendentals=TOK * FH),
    )(tokens, gate_weight, up_weight, down_weight, gate_mask, up_mask, down_mask, grad_out)
    return pl.pallas_call(
        hand_on,
        out_shape=tuple(jax.ShapeDtypeStruct(o.shape, o.dtype) for o in outs),
        in_specs=[hbm] * 5,
        out_specs=(hbm,) * 5,
        scratch_shapes=[V(o.shape, o.dtype) for o in outs] + [D((14,)), D((14,))],
        name="hand_on",
        compiler_params=pltpu.CompilerParams(vmem_limit_bytes=60 << 20),
        cost_estimate=pl.CostEstimate(flops=0, bytes_accessed=12 << 20, transcendentals=0),
    )(*outs)


def solution(mesh):
    placed = (
        P("mp", "seq"),
        P("seq", "mp"),
        P("seq", "mp"),
        P("mp", "seq"),
        P("seq", "mp"),
        P("seq", "mp"),
        P("mp", "seq"),
        P("mp", "seq"),
    )
    return jax.shard_map(
        on_device,
        mesh=mesh,
        in_specs=placed,
        out_specs=(P("mp", "seq"), P("mp", "seq"), P("seq", "mp"), P("seq", "mp"), P("mp", "seq")),
        check_vma=False,
    )
```
